512 devices in a mesh: tm: 16 (over x, z_hi, core), tok: 32 (over z_lo, y).
Axes of the slice: x: 4, y: 4, z: 16 (z_hi: 2, z_lo: 8; z = z_hi * 8 + z_lo), core: 2. Of those that a mesh axis runs over, the one named last changes fastest.
Arguments:
- queries: bfloat16 [64, 768, 1152], P('tm', 'tok'), may hold values from -6 to 6
- keys: bfloat16 [64, 768, 1152], P('tm', 'tok'), may hold values from -6 to 6
- values: bfloat16 [64, 768, 1152], P('tm', 'tok'), may hold values from -6 to 6
- out_grad: bfloat16 [64, 768, 1152], P('tm', 'tok'), may hold values from -160 to 160
- time_bias: float32 [16, 16], replicated, may hold values from 2.5 to 5.5
Outputs:
- grad_queries: bfloat16 [64, 768, 1152], P('tm', 'tok')
- grad_keys: bfloat16 [64, 768, 1152], P('tm', 'tok')
- grad_values: bfloat16 [64, 768, 1152], P('tm', 'tok')
The draws below stay inside these ranges and needn't reach their ends.
All inputs are finite; a program needn't handle non-finite values.
Results may differ from the reference program's by a relative error of at most 0.0091.
Values may be sent and summed in bfloat16 or wider, within the bound.
A program may use at most 128 MiB of HBM per device.

```python
import jax
import jax.numpy as jnp
from jax import lax

HEAD_COUNT = 16
HEAD_DIM = 72
MODEL_WIDTH = 1152
BAND_FRAMES = 8
ALL_FRAMES = 64
FRAME_TOKENS = 768


def draw_queries(key, part):
    key = jax.random.fold_in(key, 1)
    full_shape = (ALL_FRAMES, FRAME_TOKENS, MODEL_WIDTH)
    result = jnp.clip(jax.random.normal(key, full_shape, jnp.float32), -6.0, 6.0)
    return result.astype(jnp.bfloat16)


def draw_keys(key, part):
    key = jax.random.fold_in(key, 2)
    full_shape = (ALL_FRAMES, FRAME_TOKENS, MODEL_WIDTH)
    result = jnp.clip(jax.random.normal(key, full_shape, jnp.float32), -6.0, 6.0)
    return result.astype(jnp.bfloat16)


def block_scale(stream_key, dims, shards, low, largest):
    def one(axis_at, blocks):
        steps = jax.random.uniform(jax.random.fold_in(jax.random.fold_in(stream_key, 6), axis_at), (blocks,), jnp.float32, low / len(shards), largest / len(shards))
        return jnp.repeat(jnp.exp(steps), dims[axis_at] // blocks).reshape((-1,) + (1,) * (len(dims) - axis_at - 1))

    loudness = one(*shards[0])
    for cut in shards[1:]:
        loudness = loudness * one(*cut)
    return loudness


def noise(key, extent, deviation, limit, shards=(), held_as=jnp.bfloat16):
    gain = block_scale(key, extent, shards, -0.22, 0.18) if shards else 1.0
    array = jax.random.normal(key, extent, jnp.float32) * deviation * gain
    return jnp.minimum(jnp.maximum(array, -limit), limit).astype(held_as)


def setup_inputs(seed: int = 0) -> dict:
    arg_keys = jax.random.split(jax.random.key(seed), 6)
    queries = draw_queries(jax.random.fold_in(arg_keys[5], 71), 0)
    keys = draw_keys(jax.random.fold_in(arg_keys[5], 71), 0)
    values = noise(arg_keys[2], (ALL_FRAMES, FRAME_TOKENS, MODEL_WIDTH), 1.0, 6.0, ((0, 16), (1, 32)))
    out_grad = noise(arg_keys[3], (ALL_FRAMES, FRAME_TOKENS, MODEL_WIDTH), (FRAME_TOKENS ** 0.5), 160.0, ((0, 16), (1, 32)))
    time_bias = jnp.clip(jax.random.uniform(arg_keys[4], (HEAD_COUNT, 2 * BAND_FRAMES), jnp.float32, 2.5, 5.5), 2.5, 5.5)
    return dict(queries=queries, keys=keys, values=values, out_grad=out_grad, time_bias=time_bias)


def frame_shift(tensor, offset):
    padding = [(BAND_FRAMES, BAND_FRAMES)] + [(0, 0)] * (tensor.ndim - 1)
    padded = jnp.pad(tensor, padding)
    return lax.slice_in_dim(padded, BAND_FRAMES + offset, BAND_FRAMES + offset + tensor.shape[0], axis=0)


def round_half(tensor):
    return lax.optimization_barrier(tensor.astype(jnp.bfloat16)).astype(jnp.float32)


def reference(queries, keys, values, out_grad, time_bias):
    score_scale = HEAD_DIM ** -0.5
    full_shape = (ALL_FRAMES, FRAME_TOKENS, HEAD_COUNT, HEAD_DIM)
    query_heads = queries.reshape(full_shape)
    key_heads = keys.reshape(full_shape)
    value_heads = values.reshape(full_shape)
    grad_heads = out_grad.reshape(full_shape)
    query_wide = query_heads.astype(jnp.float32)
    grad_wide = grad_heads.astype(jnp.float32)
    frame_ids = jnp.arange(ALL_FRAMES)
    offsets = [offset_step for offset_step in range(-BAND_FRAMES, BAND_FRAMES + 1) if offset_step != 0]
    score_list = []
    dot_list = []
    for column, offset in enumerate(offsets):
        key_near = frame_shift(key_heads, offset).astype(jnp.float32)
        value_near = frame_shift(value_heads, offset).astype(jnp.float32)
        raw_score = jnp.einsum("fthd,fthd->fth", query_wide, key_near)
        inside = ((frame_ids + offset >= 0) & (frame_ids + offset < ALL_FRAMES))[:, None, None]
        score_list.append(jnp.where(inside, raw_score * score_scale + time_bias[:, column], -jnp.inf))
        dot_list.append(jnp.einsum("fthd,fthd->fth", grad_wide, value_near))
    score_time = jnp.stack(score_list)
    dot_time = jnp.stack(dot_list)
    pair_count = ALL_FRAMES * HEAD_COUNT

    def by_pair(tensor):
        return tensor.transpose(0, 2, 1, 3).reshape(pair_count, FRAME_TOKENS, HEAD_DIM)

    def by_pair_time(tensor):
        return tensor.transpose(1, 3, 0, 2).reshape(pair_count, len(offsets), FRAME_TOKENS)

    def spatial(item_pair):
        query_item, key_item, value_item, grad_item, score_item, dot_item = item_pair
        scores = jnp.dot(query_item, key_item.T, preferred_element_type=jnp.float32) * score_scale
        dot_values = jnp.dot(grad_item, value_item.T, preferred_element_type=jnp.float32)
        joined_max = jnp.maximum(jnp.max(scores, axis=1), jnp.max(score_item, axis=0))
        total_mass = jnp.sum(jnp.exp(scores - joined_max[:, None]), axis=1) + jnp.sum(jnp.exp(score_item - joined_max[None, :]), axis=0)
        log_total = joined_max + jnp.log(total_mass)
        weights = jnp.exp(scores - log_total[:, None])
        weights_time = jnp.exp(score_item - log_total[None, :])
        delta_value = jnp.sum(weights * dot_values, axis=1) + jnp.sum(weights_time * dot_item, axis=0)
        rounded = lax.optimization_barrier(weights.astype(jnp.bfloat16))
        slopes = (rounded.astype(jnp.float32) * (dot_values - delta_value[:, None])).astype(jnp.bfloat16)
        grad_query = jnp.dot(slopes, key_item, preferred_element_type=jnp.float32) * score_scale
        grad_key = jnp.dot(slopes.T, query_item, preferred_element_type=jnp.float32) * score_scale
        grad_value = jnp.dot(rounded.T, grad_item, preferred_element_type=jnp.float32)
        return grad_query, grad_key, grad_value, log_total, delta_value

    mapped = lax.map(spatial, (by_pair(query_heads), by_pair(key_heads), by_pair(value_heads), by_pair(grad_heads), by_pair_time(score_time), by_pair_time(dot_time)))

    def unpair(tensor):
        return tensor.reshape(ALL_FRAMES, HEAD_COUNT, FRAME_TOKENS, HEAD_DIM).transpose(0, 2, 1, 3)

    def unpair_rows(tensor):
        return tensor.reshape(ALL_FRAMES, HEAD_COUNT, FRAME_TOKENS).transpose(0, 2, 1)

    grad_query = unpair(mapped[0])
    grad_key = unpair(mapped[1])
    grad_value = unpair(mapped[2])
    log_total = unpair_rows(mapped[3])
    delta_value = unpair_rows(mapped[4])
    for column, offset in enumerate(offsets):
        rounded = round_half(jnp.exp(score_time[column] - log_total))
        slope_value = round_half(rounded * (dot_time[column] - delta_value))
        key_near = frame_shift(key_heads, offset).astype(jnp.float32)
        grad_query = grad_query + score_scale * slope_value[..., None] * key_near
        grad_key = grad_key + frame_shift(score_scale * slope_value[..., None] * query_wide, -offset)
        grad_value = grad_value + frame_shift(rounded[..., None] * grad_wide, -offset)
    out_shape = (ALL_FRAMES, FRAME_TOKENS, MODEL_WIDTH)
    return (grad_query.reshape(out_shape).astype(jnp.bfloat16), grad_key.reshape(out_shape).astype(jnp.bfloat16), grad_value.reshape(out_shape).astype(jnp.bfloat16))
```

```python
import functools

import jax
import jax.numpy as jnp
from jax import lax
from jax.experimental import pallas as pl
from jax.experimental.pallas import tpu as pltpu
from jax.sharding import PartitionSpec as P

F32 = jnp.float32
BF16 = jnp.bfloat16
HEADS = 16
DIM = 72
TOKENS = 24
FRAMES = 4
WIDTH = HEADS * DIM
BAND = 8
GROUPS = 32
ROWS = GROUPS * TOKENS
PAIR = 2 * TOKENS
FWD = 112
BWD = 96
SCALE = DIM**-0.5
NT = (((1,), (1,)), ((), ()))


def device(x, z, core, y):
    return (x * 4 + lax.div(z, 8) * 2 + core, lax.rem(z, 8) * 4 + y)


def lanes_of(rows):
    return lax.broadcasted_iota(jnp.int32, (rows, 128), 1)


def pieces(source, target, width):
    found = []
    while width:
        step = min(width, 128 - source % 128, 128 - target % 128)
        low = target % 128
        found.append((source // 128, (target - source) % 128, low, low + step))
        source, target, width = source + step, target + step, width - step
    return found


def moved(value, shift):
    return value if shift == 0 else pltpu.roll(value, shift, 1)


def assemble(lane, parts):
    result = None
    for value, shift, low, high in reversed(parts):
        piece = moved(value, shift)
        result = piece if result is None else jnp.where(lane < high, piece, result)
    return result


def pack_heads(refs, send):
    def one_pair(pair, _):
        lane = lanes_of(PAIR)
        lane16 = lanes_of(16)
        tiles = []
        for ref in refs:
            wide = [ref[2 * pair + j].astype(F32) for j in range(2)]
            tiles.append(
                [
                    jnp.concatenate([w[:, 128 * t : 128 * t + 128] for w in wide], axis=0)
                    for t in range(WIDTH // 128)
                ]
            )
        for head in range(HEADS):
            start = head * DIM

            def run(array, first, target, width):
                return [
                    (tiles[array][t], s, a, b)
                    for t, s, a, b in pieces(start + first, target, width)
                ]

            upper = assemble(lane, run(0, 0, 0, 72) + run(1, 0, 72, 56))
            lower = assemble(lane, run(1, 56, 0, 16) + run(2, 0, 16, 72) + run(3, 0, 88, 40))
            rest = []
            for r in range(3):
                for value, s, a, b in run(3, 40, 32 * r, 32):
                    rest.append((value[16 * r : 16 * r + 16], s, a, b))
            rest = assemble(lane16, rest)
            send[head, pair, 0:48, :] = upper.astype(BF16)
            send[head, pair, 48:96, :] = lower.astype(BF16)
            send[head, pair, 96:112, :] = rest.astype(BF16)
        return 0

    lax.fori_loop(0, 2, one_pair, 0)


def unpack_blocks(block, q_ref, k_ref, v_ref, g_ref):
    def one(i, _):
        lane = lanes_of(PAIR)
        upper = block(i, 0, 48).astype(F32)
        lower = block(i, 48, 48).astype(F32)
        rest = block(i, 96, 16).astype(F32)
        q = jnp.where(lane < DIM, upper, 0.0)
        k = pltpu.roll(jnp.where(lane >= DIM, upper, lower), 56, 1)
        v = pltpu.roll(lower, 112, 1)
        tail = jnp.concatenate([pltpu.roll(rest, 40 - 32 * r + (128 if r == 2 else 0), 1) for r in range(3)], axis=0)
        g = jnp.where(lane < 40, pltpu.roll(lower, 40, 1), jnp.where(lane < DIM, tail, 0.0))
        for j in range(2):
            at = pl.ds(pl.multiple_of(j * ROWS + i * TOKENS, 8), TOKENS)
            part = slice(j * TOKENS, (j + 1) * TOKENS)
            q_ref[at, :] = q[part]
            k_ref[at, :] = k[part]
            v_ref[at, :] = v[part]
            g_ref[at, :] = g[part]
        return 0

    lax.fori_loop(0, GROUPS, one, 0)


def pack_grads(dq, dk, dv):
    lane = lanes_of(dq.shape[0])
    turned = pltpu.roll(dk, 72, 1)
    upper = jnp.where(lane < 72, dq, turned)
    lower = jnp.where(lane < 16, turned, pltpu.roll(dv, 16, 1))
    return upper, lower


def store_grads(upper_ref, lower_ref, out):
    def one(i, _):
        for n, ref in enumerate((upper_ref, lower_ref)):
            both = [
                ref[pl.ds(pl.multiple_of(j * ROWS + i * TOKENS, 8), TOKENS), :] for j in range(2)
            ]
            out[i, 48 * n : 48 * n + 48, :] = jnp.concatenate(both, axis=0).astype(BF16)
        return 0

    lax.fori_loop(0, GROUPS, one, 0)


def combine(m1, l1, s1, m2, l2, s2):
    top = jnp.maximum(m1, m2)
    a1 = jnp.exp(m1 - top)
    a2 = jnp.exp(m2 - top)
    mass = l1 * a1 + l2 * a2
    return a1 / mass, (s1 * a1 + s2 * a2) / mass


def kernel(
    q_in, k_in, v_in, g_in, bias_ref, dq_out, dk_out, dv_out,
    send, plane, spat, temp,
    qs, ks, vs, gs, qt, kt, vt, gt,
    e_s, d_s, p_s, sl_s, e_t, d_t,
    stat_s, stat_t, to_t, to_s, from_s, from_t,
    grad_s, grad_t, back_s, back_t, final, landed,
    z_send, z_recv, y_send, y_recv, x_send, x_recv,
    ts_send, ts_recv, st_send, st_recv,
    bx_send, bx_recv, by_send, by_recv, bz_send, bz_recv,
):
    tm = lax.axis_index("tm")
    tok = lax.axis_index("tok")
    x, zhi, core = lax.div(tm, 4), lax.rem(lax.div(tm, 2), 2), lax.rem(tm, 2)
    zlo, y = lax.div(tok, 4), lax.rem(tok, 4)
    z = zhi * 8 + zlo
    spot = x * 2 + core
    my_pair = x * 8 + lax.div(y, 2) * 4 + core * 2 + lax.rem(y, 2)
    my_group = y * 8 + spot

    def remote(src, dst, s_sem, r_sem, target):
        return pltpu.make_async_remote_copy(
            src_ref=src, dst_ref=dst, send_sem=s_sem, recv_sem=r_sem,
            device_id=target, device_id_type=pl.DeviceIdType.MESH,
        )

    def start(src, dst, s_sem, r_sem, target, here):
        @pl.when(here)
        def _():
            pltpu.make_async_copy(src, dst, r_sem).start()

        @pl.when(jnp.logical_not(here))
        def _():
            remote(src, dst, s_sem, r_sem, target).start()

    def arrived(ref, sem):
        pltpu.make_async_copy(ref, ref, sem).wait()

    def sent(ref, sem, here):
        @pl.when(jnp.logical_not(here))
        def _():
            pltpu.make_async_copy(ref, ref, sem).wait()

    barrier = pltpu.get_barrier_semaphore()

    def hail_line(d, _):
        pl.semaphore_signal(
            barrier, inc=1, device_id=device(x, lax.rem(z + d, 16), core, y),
            device_id_type=pl.DeviceIdType.MESH,
        )
        return 0

    lax.fori_loop(1, 16, hail_line, 0)
    place = y * 8 + spot

    def hail_plane(d, _):
        other = lax.rem(place + d, 32)
        there = lax.rem(other, 8)
        pl.semaphore_signal(
            barrier, inc=1,
            device_id=device(lax.div(there, 2), z, lax.rem(there, 2), lax.div(other, 8)),
            device_id_type=pl.DeviceIdType.MESH,
        )
        return 0

    lax.fori_loop(1, 32, hail_plane, 0)
    pack_heads((q_in, k_in, v_in, g_in), send)
    pl.semaphore_wait(barrier, 46)

    pltpu.make_async_copy(send.at[z], plane.at[z], z_recv.at[z]).start()

    def send_line(n, _):
        d = jnp.where(lax.rem(n, 2) == 1, lax.div(n + 1, 2), 16 - lax.div(n, 2))
        to = lax.rem(z + d, 16)
        remote(
            send.at[to], plane.at[z], z_send.at[to], z_recv.at[z], device(x, to, core, y)
        ).start()
        return 0

    lax.fori_loop(1, 16, send_line, 0)

    def forward(n, _):
        d = jnp.where(lax.rem(n, 2) == 1, 16 - lax.div(n + 1, 2), lax.div(n, 2))
        source = lax.rem(z + d, 16)
        hi, lo = lax.div(source, 8), lax.rem(source, 8)
        arrived(plane.at[source], z_recv.at[source])
        to_x, to_core = lax.div(lo, 2), lax.rem(lo, 2)
        start(
            plane.at[source], temp.at[4 * x + 2 * hi + core],
            x_send.at[source], x_recv.at[4 * x + 2 * hi + core],
            device(to_x, z, to_core, y), lo == spot,
        )
        for p in range(2):
            to_y = 2 * hi + p
            start(
                plane.at[source, p], spat.at[y * 8 + lo],
                y_send.at[2 * source + p], y_recv.at[y * 8 + lo],
                device(x, z, core, to_y), to_y == y,
            )
        return 0

    lax.fori_loop(0, 16, forward, 0)

    def wait_x(n, _):
        arrived(temp.at[n], x_recv.at[n])
        return 0

    lax.fori_loop(0, 16, wait_x, 0)
    unpack_blocks(
        lambda i, a, n: temp[lax.div(i, 2), lax.rem(i, 2), a : a + n, :], qt, kt, vt, gt
    )
    frame_k = lax.broadcasted_iota(jnp.int32, (64, 64), 0)
    frame_q = lax.broadcasted_iota(jnp.int32, (64, 64), 1)
    frame_k = 2 * lax.rem(frame_k, 32) + lax.div(frame_k, 32)
    frame_q = 2 * lax.rem(frame_q, 32) + lax.div(frame_q, 32)
    offset = frame_k - frame_q
    bias = jnp.full((64, 64), -jnp.inf, F32)
    for j in range(2 * BAND):
        o = j - BAND if j < BAND else j - BAND + 1
        bias = jnp.where(offset == o, bias_ref[z, j], bias)
    stat_t[...] = jnp.zeros_like(stat_t)
    for t in range(TOKENS):
        at = pl.ds(t, 64, stride=TOKENS)
        s = lax.dot_general(
            kt[at, :].astype(BF16), qt[at, :].astype(BF16), NT, preferred_element_type=F32
        ) * SCALE + bias
        d = lax.dot_general(
            vt[at, :].astype(BF16), gt[at, :].astype(BF16), NT, preferred_element_type=F32
        )
        top = jnp.max(s, axis=0, keepdims=True)
        e = jnp.exp(s - top)
        e_t[t] = e
        d_t[t] = d
        stat_t[t : t + 1, 0:64] = top
        stat_t[24 + t : 25 + t, 0:64] = jnp.sum(e, axis=0, keepdims=True)
        stat_t[48 + t : 49 + t, 0:64] = jnp.sum(e * d, axis=0, keepdims=True)
    turned = stat_t[...].T
    to_s[...] = jnp.zeros_like(to_s)
    for j in range(2):
        to_s[pl.ds(j, 32, stride=8), :] = turned[32 * j : 32 * j + 32]

    def send_ts(n, _):
        r = lax.rem(my_pair + n, 32)
        rx, rh, rc, rp = (
            lax.div(r, 8), lax.rem(lax.div(r, 4), 2), lax.rem(lax.div(r, 2), 2), lax.rem(r, 2),
        )
        start(
            to_s.at[pl.ds(pl.multiple_of(r * 8, 8), 8)],
            from_t.at[pl.ds(pl.multiple_of(my_group * 8, 8), 8)],
            ts_send.at[r], ts_recv.at[my_group], device(rx, z, rc, 2 * rh + rp), r == my_pair,
        )
        return 0

    lax.fori_loop(0, 32, send_ts, 0)

    def wait_y(n, _):
        arrived(spat.at[n], y_recv.at[n])
        return 0

    lax.fori_loop(0, 32, wait_y, 0)
    unpack_blocks(lambda i, a, n: spat[i, a : a + n, :], qs, ks, vs, gs)
    stat_s[...] = jnp.zeros_like(stat_s)

    def scores(n, _):
        j, b = lax.div(n, 3), lax.rem(n, 3)
        keys_at = pl.ds(pl.multiple_of(j * ROWS, 8), ROWS)
        rows_at = pl.ds(pl.multiple_of(j * ROWS + b * 256, 8), 256)
        lanes_at = pl.ds(pl.multiple_of(b * 256, 128), 256)
        s = lax.dot_general(
            ks[keys_at, :].astype(BF16), qs[rows_at, :].astype(BF16), NT,
            preferred_element_type=F32,
        ) * SCALE
        d = lax.dot_general(
            vs[keys_at, :].astype(BF16), gs[rows_at, :].astype(BF16), NT,
            preferred_element_type=F32,
        )
        top = jnp.max(s, axis=0, keepdims=True)
        e = jnp.exp(s - top)
        e_s[j, :, lanes_at] = e
        d_s[j, :, lanes_at] = d
        stat_s[pl.ds(j, 1), lanes_at] = top
        stat_s[pl.ds(2 + j, 1), lanes_at] = jnp.sum(e, axis=0, keepdims=True)
        stat_s[pl.ds(4 + j, 1), lanes_at] = jnp.sum(e * d, axis=0, keepdims=True)
        return 0

    lax.fori_loop(0, 6, scores, 0)
    stat = stat_s[...]
    row = lax.broadcasted_iota(jnp.int32, (256, ROWS), 0)
    lane = lax.broadcasted_iota(jnp.int32, (256, ROWS), 1)
    spread = jnp.where(
        lax.div(lane, TOKENS) == lax.div(row, 8), jnp.concatenate([stat] * 32, axis=0), 0.0
    )
    row = lax.broadcasted_iota(jnp.int32, (ROWS, 128), 0)
    lane = lax.broadcasted_iota(jnp.int32, (ROWS, 128), 1)
    pick = (lax.rem(row, TOKENS) == lane).astype(F32)
    to_t[...] = jnp.dot(
        spread, pick, precision=lax.Precision.HIGHEST, preferred_element_type=F32
    )

    def send_st(n, _):
        i = lax.rem(my_group + n, 32)
        iy, lo = lax.div(i, 8), lax.rem(i, 8)
        start(
            to_t.at[pl.ds(pl.multiple_of(i * 8, 8), 8)],
            from_s.at[pl.ds(pl.multiple_of(my_pair * 8, 8), 8)],
            st_send.at[i], st_recv.at[my_pair],
            device(lax.div(lo, 2), z, lax.rem(lo, 2), iy), i == my_group,
        )
        return 0

    lax.fori_loop(0, 32, send_st, 0)

    def wait_stats(n, _):
        at = pl.ds(pl.multiple_of(n * 8, 8), 8)
        arrived(from_t.at[at], ts_recv.at[n])
        arrived(from_s.at[at], st_recv.at[n])
        return 0

    lax.fori_loop(0, 32, wait_stats, 0)

    theirs = [
        jnp.concatenate(
            [from_s[pl.ds(2 * n + j, 32, stride=8), :] for j in range(2)], axis=0
        ).T[0:TOKENS]
        for n in range(3)
    ]
    mine = [stat_t[24 * n : 24 * n + 24, 0:64] for n in range(3)]
    scale_t, delta_t = combine(*mine, *theirs)
    for t in range(TOKENS):
        at = pl.ds(t, 64, stride=TOKENS)
        rounded = (e_t[t] * scale_t[t : t + 1]).astype(BF16)
        slope = (rounded.astype(F32) * (d_t[t] - delta_t[t : t + 1])).astype(BF16)
        k = kt[at, :].astype(BF16)
        q = qt[at, :].astype(BF16)
        g = gt[at, :].astype(BF16)
        dk = jnp.dot(slope, q, preferred_element_type=F32) * SCALE
        dv = jnp.dot(rounded, g, preferred_element_type=F32)
        across = slope.astype(F32).T.astype(BF16)
        dq = jnp.dot(across, k, preferred_element_type=F32) * SCALE
        upper, lower = pack_grads(dq, dk, dv)
        qt[at, :] = upper
        vt[at, :] = lower
    store_grads(qt, vt, grad_t)

    def send_bx(n, _):
        hi, place_x = lax.rem(n, 2), lax.rem(spot + lax.div(n, 2), 8)
        to_x, to_core = lax.div(place_x, 2), lax.rem(place_x, 2)
        block = pl.ds(pl.multiple_of(2 * (4 * to_x + 2 * hi + to_core), 2), 2)
        source = hi * 8 + spot
        start(
            grad_t.at[block], back_t.at[source],
            bx_send.at[hi * 8 + place_x], bx_recv.at[source],
            device(to_x, z, to_core, y), place_x == spot,
        )
        return 0

    lax.fori_loop(0, 16, send_bx, 0)

    lane = lax.broadcasted_iota(jnp.int32, (64, ROWS), 1)
    row = lax.broadcasted_iota(jnp.int32, (64, ROWS), 0)
    own = lax.div(lane, TOKENS) == lax.rem(row, 32)
    got = jnp.concatenate([from_t[pl.ds(j, 32, stride=8), :] for j in range(2)], axis=0)
    theirs = []
    lane = lax.broadcasted_iota(jnp.int32, (128, ROWS), 1)
    row = lax.broadcasted_iota(jnp.int32, (128, ROWS), 0)
    for n in range(3):
        repeat = (lax.rem(lane, TOKENS) == row - TOKENS * n).astype(F32)
        wide = jnp.dot(
            got, repeat, precision=lax.Precision.HIGHEST, preferred_element_type=F32
        )
        wide = jnp.where(own, wide, 0.0)
        theirs.append(
            jnp.concatenate(
                [jnp.sum(wide[32 * j : 32 * j + 32], axis=0, keepdims=True) for j in range(2)],
                axis=0,
            )
        )
    mine = [stat[2 * n : 2 * n + 2] for n in range(3)]
    scale_s, delta_s = combine(*mine, *theirs)
    stat_s[0:2, :] = scale_s
    stat_s[2:4, :] = delta_s

    def slopes(n, _):
        j, b = lax.div(n, 3), lax.rem(n, 3)
        lanes_at = pl.ds(pl.multiple_of(b * 256, 128), 256)
        rounded = (e_s[j, :, lanes_at] * stat_s[pl.ds(j, 1), lanes_at]).astype(BF16)
        gap = d_s[j, :, lanes_at] - stat_s[pl.ds(2 + j, 1), lanes_at]
        p_s[j, :, lanes_at] = rounded
        sl_s[j, :, lanes_at] = (rounded.astype(F32) * gap).astype(BF16)
        return 0

    lax.fori_loop(0, 6, slopes, 0)

    def grads(j, _):
        rows_at = pl.ds(pl.multiple_of(j * ROWS, 8), ROWS)
        q = qs[rows_at, :].astype(BF16)
        g = gs[rows_at, :].astype(BF16)
        k_turned = ks[rows_at, :].T.astype(BF16)
        dk = jnp.dot(sl_s[j], q, preferred_element_type=F32) * SCALE
        dv = jnp.dot(p_s[j], g, preferred_element_type=F32)
        dq = jnp.dot(k_turned, sl_s[j], preferred_element_type=F32).T * SCALE
        upper, lower = pack_grads(dq, dk, dv)
        qs[rows_at, :] = upper
        vs[rows_at, :] = lower
        return 0

    lax.fori_loop(0, 2, grads, 0)
    store_grads(qs, vs, grad_s)

    def send_by(n, _):
        to_y = lax.rem(y + n, 4)
        start(
            grad_s.at[pl.ds(pl.multiple_of(to_y * 8, 8), 8)], back_s.at[y],
            by_send.at[to_y], by_recv.at[y], device(x, z, core, to_y), to_y == y,
        )
        return 0

    lax.fori_loop(0, 4, send_by, 0)

    def wait_bx(n, _):
        arrived(back_t.at[n], bx_recv.at[n])
        return 0

    lax.fori_loop(0, 16, wait_bx, 0)

    def wait_by(n, _):
        arrived(back_s.at[n], by_recv.at[n])
        return 0

    lax.fori_loop(0, 4, wait_by, 0)

    def send_home(n, _):
        d = jnp.where(lax.rem(n, 2) == 1, lax.div(n + 1, 2), 16 - lax.div(n, 2))
        to = lax.rem(z + d, 16)
        hi, lo = lax.div(to, 8), lax.rem(to, 8)
        for p in range(2):
            total = back_s[2 * hi + p, lo].astype(F32) + back_t[to, p].astype(F32)
            final[to, p] = total.astype(BF16)
        start(
            final.at[to], landed.at[z], bz_send.at[to], bz_recv.at[z],
            device(x, to, core, y), to == z,
        )
        return 0

    lax.fori_loop(0, 16, send_home, 0)

    def wait_home(n, _):
        arrived(landed.at[n], bz_recv.at[n])
        return 0

    lax.fori_loop(0, 16, wait_home, 0)

    def restore(pair, _):
        lane = lanes_of(PAIR)
        runs = [[[] for _ in range(WIDTH // 128)] for _ in range(3)]
        for head in range(HEADS):
            upper = landed[head, pair, 0:48, :].astype(F32)
            lower = landed[head, pair, 48:96, :].astype(F32)
            start_lane = head * DIM
            for array, value, source, first, width in (
                (0, upper, 0, 0, 72), (1, upper, 72, 0, 56), (1, lower, 0, 56, 16),
                (2, lower, 16, 0, 72),
            ):
                target = start_lane + first
                while width:
                    step = min(width, 128 - target % 128)
                    low = target % 128
                    runs[array][target // 128].append(
                        (value, (low - source) % 128, low, low + step)
                    )
                    source, target, width = source + step, target + step, width - step
        for array, out in enumerate((dq_out, dk_out, dv_out)):
            for t in range(WIDTH // 128):
                whole = assemble(lane, runs[array][t])
                for j in range(2):
                    out[2 * pair + j, :, 128 * t : 128 * t + 128] = whole[
                        TOKENS * j : TOKENS * j + TOKENS
                    ].astype(BF16)
        return 0

    lax.fori_loop(0, 2, restore, 0)

    def drain(n, _):
        @pl.when(n != z)
        def _():
            pltpu.make_async_copy(send.at[n], send.at[n], z_send.at[n]).wait()
            pltpu.make_async_copy(final.at[n], final.at[n], bz_send.at[n]).wait()

        hi, lo = lax.div(n, 8), lax.rem(n, 8)
        sent(plane.at[n], x_send.at[n], lo == spot)
        sent(back_t.at[n], bx_send.at[n], lo == spot)
        for p in range(2):
            sent(plane.at[n, p], y_send.at[2 * n + p], 2 * hi + p == y)
        return 0

    lax.fori_loop(0, 16, drain, 0)

    def drain_stats(n, _):
        at = pl.ds(pl.multiple_of(n * 8, 8), 8)
        sent(to_s.at[at], ts_send.at[n], n == my_pair)
        sent(to_t.at[at], st_send.at[n], n == my_group)
        return 0

    lax.fori_loop(0, 32, drain_stats, 0)

    def drain_y(n, _):
        sent(back_s.at[n], by_send.at[n], n == y)
        return 0

    lax.fori_loop(0, 4, drain_y, 0)


def body(queries, keys, values, out_grad, time_bias):
    vmem = pl.BlockSpec(memory_space=pltpu.VMEM)
    shape = jax.ShapeDtypeStruct(queries.shape, BF16)
    wide = pltpu.VMEM((2 * ROWS, 128), F32)
    dma = pltpu.SemaphoreType.DMA
    return pl.pallas_call(
        kernel,
        out_shape=(shape, shape, shape),
        in_specs=[vmem] * 4 + [pl.BlockSpec(memory_space=pltpu.SMEM)],
        out_specs=(vmem, vmem, vmem),
        scratch_shapes=[
            pltpu.VMEM((16, 2, FWD, 128), BF16),
            pltpu.VMEM((16, 2, FWD, 128), BF16),
            pltpu.VMEM((32, FWD, 128), BF16),
            pltpu.VMEM((16, 2, FWD, 128), BF16),
            wide, wide, wide, wide, wide, wide, wide, wide,
            pltpu.VMEM((2, ROWS, ROWS), F32),
            pltpu.VMEM((2, ROWS, ROWS), F32),
            pltpu.VMEM((2, ROWS, ROWS), BF16),
            pltpu.VMEM((2, ROWS, ROWS), BF16),
            pltpu.VMEM((TOKENS, 64, 64), F32),
            pltpu.VMEM((TOKENS, 64, 64), F32),
            pltpu.VMEM((8, ROWS), F32),
            pltpu.VMEM((128, 128), F32),
            pltpu.VMEM((256, 128), F32),
            pltpu.VMEM((256, 128), F32),
            pltpu.VMEM((256, 128), F32),
            pltpu.VMEM((256, 128), F32),
            pltpu.VMEM((32, BWD, 128), BF16),
            pltpu.VMEM((32, BWD, 128), BF16),
            pltpu.VMEM((4, 8, BWD, 128), BF16),
            pltpu.VMEM((16, 2, BWD, 128), BF16),
            pltpu.VMEM((16, 2, BWD, 128), BF16),
            pltpu.VMEM((16, 2, BWD, 128), BF16),
            dma((16,)), dma((16,)), dma((32,)), dma((32,)), dma((16,)), dma((16,)),
            dma((32,)), dma((32,)), dma((32,)), dma((32,)),
            dma((16,)), dma((16,)), dma((4,)), dma((4,)), dma((16,)), dma((16,)),
        ],
        compiler_params=pltpu.CompilerParams(
            collective_id=0, has_side_effects=True, vmem_limit_bytes=56 * 2**20
        ),
    )(queries, keys, values, out_grad, time_bias)


def solution(mesh):
    spec = P("tm", "tok", None)
    return jax.shard_map(
        body, mesh=mesh, in_specs=(spec, spec, spec, spec, P()),
        out_specs=(spec, spec, spec), check_vma=False,
    )
```

```python
import jax
import jax.numpy as jnp
from jax import lax
from jax.experimental import pallas as pl
from jax.experimental.pallas import tpu as pltpu
from jax.sharding import PartitionSpec as P

F32 = jnp.float32
BF16 = jnp.bfloat16
HEADS = 16
DIM = 72
TOKENS = 24
WIDTH = HEADS * DIM
BAND = 8
GROUPS = 32
ROWS = GROUPS * TOKENS
PAIR = 2 * TOKENS
SCALE = DIM**-0.5
NT = (((1,), (1,)), ((), ()))
HIGHEST = lax.Precision.HIGHEST


def device(x, z, core, y):
    return (x * 4 + lax.div(z, 8) * 2 + core, lax.rem(z, 8) * 4 + y)


def lanes_of(rows):
    return lax.broadcasted_iota(jnp.int32, (rows, 128), 1)


def turn(value, shift):
    if isinstance(shift, int):
        shift %= 128
        return value if shift == 0 else pltpu.roll(value, shift, 1)
    return pltpu.roll(value, lax.rem(shift + 256, 128), 1)


def group(value, r):
    return value[16 * r : 16 * r + 16]


def head_run(ref, pair, head):
    first, offset = head * DIM // 128, head * DIM % 128
    tile = [
        jnp.concatenate(
            [ref[2 * pair + j, :, 128 * t : 128 * t + 128].astype(F32) for j in range(2)], axis=0
        )
        for t in range(first, first + (2 if offset + DIM > 128 else 1))
    ]
    if len(tile) == 1:
        return tile[0], offset
    return jnp.where(lanes_of(PAIR) >= offset, tile[0], tile[1]), offset


def pack_first(q_in, k_in, out):
    lane, lane16 = lanes_of(PAIR), lanes_of(16)
    for head in range(HEADS):
        extra = None
        for pair in range(2):
            q, at = head_run(q_in, pair, head)
            k, _ = head_run(k_in, pair, head)
            k = turn(k, 72 - at)
            main = jnp.where(lane < DIM, turn(q, -at), k).astype(BF16)
            for r in range(3):
                out[head, 4 * pair + r] = group(main, r)
                low = 16 * (3 * pair + r)
                piece = turn(group(k, r), low)
                extra = piece if extra is None else jnp.where(lane16 >= low, piece, extra)
        out[head, 3] = extra.astype(BF16)


def pack_second(g_in, v_in, out_g, out_v):
    lane16 = lanes_of(16)
    half = lane16 < 64
    for head in range(HEADS):
        extra = None
        shared_g, shared_v = [], []
        for pair in range(2):
            g, at = head_run(g_in, pair, head)
            v, _ = head_run(v_in, pair, head)
            g = turn(g, -at)
            v = turn(v, -at - 8)
            out_g[head, 3 * pair] = jnp.where(half, group(g, 0), turn(group(g, 1), 64)).astype(BF16)
            out_v[head, 2 * pair] = jnp.where(half, group(v, 0), turn(group(v, 1), 64)).astype(BF16)
            shared_g.append(group(g, 2))
            shared_v.append(group(v, 2))
            for r in range(3):
                low = 16 * (3 * pair + r)
                piece = turn(group(g, r), low - 64)
                extra = piece if extra is None else jnp.where(lane16 >= low, piece, extra)
                extra = jnp.where(lane16 >= low + 8, turn(group(v, r), low + 16), extra)
        out_g[head, 1] = jnp.where(half, shared_g[0], turn(shared_g[1], 64)).astype(BF16)
        out_v[head, 1] = jnp.where(half, shared_v[0], turn(shared_v[1], 64)).astype(BF16)
        out_g[head, 2] = extra.astype(BF16)


def store_rows(ref, i, value):
    for j in range(2):
        at = pl.ds(pl.multiple_of(j * ROWS + i * TOKENS, 8), TOKENS)
        ref[at, :] = value[j * TOKENS : (j + 1) * TOKENS]


def load_rows(ref, i):
    return jnp.concatenate(
        [
            ref[pl.ds(pl.multiple_of(j * ROWS + i * TOKENS, 8), TOKENS), :]
            for j in range(2)
        ],
        axis=0,
    )


def unpack_first(tile, pair_of, q_ref, k_ref):
    def one(i, _):
        lane = lanes_of(PAIR)
        p = pair_of(i)
        main = jnp.concatenate([tile(i, r + p).astype(F32) for r in range(3)], axis=0)
        extra = tile(i, 3 - 3 * p).astype(F32)
        extra = jnp.concatenate([turn(extra, -48 * p - 16 * r) for r in range(3)], axis=0)
        store_rows(q_ref, i, jnp.where(lane < DIM, main, 0.0))
        store_rows(k_ref, i, turn(jnp.where(lane >= DIM, main, extra), 56))
        return 0

    lax.fori_loop(0, GROUPS, one, 0)


def unpack_second(tile, pair_of, g_ref):
    def one(i, _):
        lane = lanes_of(PAIR)
        p = pair_of(i)
        own = tile(i, 2 * p).astype(F32)
        shared = tile(i, 1 - p).astype(F32)
        extra = tile(i, 2 - p).astype(F32)
        main = jnp.concatenate([own, turn(own, 64), turn(shared, 64 * p)], axis=0)
        tail = jnp.concatenate([turn(extra, 64 - 48 * p - 16 * r) for r in range(3)], axis=0)
        store_rows(g_ref, i, jnp.where(lane < 64, main, jnp.where(lane < DIM, tail, 0.0)))
        return 0

    lax.fori_loop(0, GROUPS, one, 0)


def unpack_third(tile, tile_g, pair_of, v_ref):
    def one(i, _):
        lane = lanes_of(PAIR)
        p = pair_of(i)
        own = tile(i, p).astype(F32)
        shared = tile(i, 1 - p).astype(F32)
        extra = tile_g(i, 2 - p).astype(F32)
        main = jnp.concatenate([turn(own, 8), turn(own, 72), turn(shared, 8 - 64 * p)], axis=0)
        head = jnp.concatenate([turn(extra, -8 - 48 * p - 16 * r) for r in range(3)], axis=0)
        store_rows(v_ref, i, jnp.where(lane < 8, head, jnp.where(lane < DIM, main, 0.0)))
        return 0

    lax.fori_loop(0, GROUPS, one, 0)


def value_tiles(dv, p):
    lane16 = lanes_of(16)
    half = lane16 < 64
    own = jnp.where(half, group(dv, 0), turn(group(dv, 1), 64))
    shared = turn(jnp.where(half, group(dv, 2), 0.0), 64 * p)
    extra = jnp.zeros_like(own)
    for r in reversed(range(3)):
        inside = (lane16 >= 16 * r) & (lane16 < 16 * r + 8)
        extra = jnp.where(inside, turn(group(dv, r), 16 * r - 64), extra)
    return own, shared, turn(extra, 48 * p)


def key_tiles(dq, dk, p):
    lane, lane16 = lanes_of(PAIR), lanes_of(16)
    dk = turn(dk, 72)
    main = jnp.where(lane < DIM, dq, dk)
    extra = jnp.zeros((16, 128), F32)
    for r in range(3):
        inside = (lane16 >= 16 * r) & (lane16 < 16 * r + 16)
        extra = jnp.where(inside, turn(group(dk, r), 16 * r), extra)
    return [group(main, r) for r in range(3)], turn(extra, 48 * p)


def spread_heads(parts, out, pair):
    lane = lanes_of(PAIR)
    for t in range(WIDTH // 128):
        whole = None
        for head in reversed(range(HEADS)):
            low, high = head * DIM - 128 * t, head * DIM + DIM - 128 * t
            if high <= 0 or low >= 128:
                continue
            whole = parts[head] if whole is None else jnp.where(lane < high, parts[head], whole)
        for j in range(2):
            out[2 * pair + j, :, 128 * t : 128 * t + 128] = whole[
                TOKENS * j : TOKENS * j + TOKENS
            ].astype(BF16)


def restore_values(landed, dv_out):
    for pair in range(2):
        parts = []
        lane = lanes_of(PAIR)
        for head in range(HEADS):
            own = landed[head, 3 * pair].astype(F32)
            shared = landed[head, 1].astype(F32)
            extra = landed[head, 2].astype(F32)
            main = jnp.concatenate([own, turn(own, 64), turn(shared, 64 * pair)], axis=0)
            tail = jnp.concatenate(
                [turn(extra, 64 - 48 * pair - 16 * r) for r in range(3)], axis=0
            )
            parts.append(turn(jnp.where(lane < 64, main, tail), head * DIM))
        spread_heads(parts, dv_out, pair)


def restore_keys(landed, dq_out, dk_out):
    for pair in range(2):
        lane = lanes_of(PAIR)
        q_parts, k_parts = [], []
        for head in range(HEADS):
            main = jnp.concatenate(
                [landed[head, 4 * pair + r].astype(F32) for r in range(3)], axis=0
            )
            extra = landed[head, 3].astype(F32)
            extra = jnp.concatenate([turn(extra, -48 * pair - 16 * r) for r in range(3)], axis=0)
            q_parts.append(turn(main, head * DIM))
            k_parts.append(turn(jnp.where(lane >= DIM, main, extra), head * DIM - DIM))
        spread_heads(q_parts, dq_out, pair)
        spread_heads(k_parts, dk_out, pair)


def far_step(n):
    return jnp.where(lax.rem(n, 2) == 1, 8 + lax.div(n, 2), 8 - lax.div(n, 2))


def scratch():
    dma = pltpu.SemaphoreType.DMA

    def tiles(blocks, count):
        return pltpu.VMEM((blocks, count, 16, 128), BF16)

    wide = pltpu.VMEM((2 * ROWS, 128), F32)
    square = (2, ROWS, ROWS)
    small = (TOKENS, 64, 64)
    shapes = {}
    for n, (whole, part) in {1: (7, 4), 2: (4, 3), 3: (3, 2)}.items():
        shapes[f"send{n}"] = tiles(16, whole)
        shapes[f"plane{n}"] = tiles(16, whole)
        shapes[f"temp{n}"] = tiles(16, whole)
        shapes[f"spat{n}"] = tiles(32, part)
        for name, count in (("zs", 16), ("zr", 16), ("xs", 16), ("xr", 16), ("ys", 32), ("yr", 32)):
            shapes[f"{name}{n}"] = dma((count,))
    for n, (whole, part) in {"v": (4, 3), "k": (7, 4)}.items():
        shapes[f"grad_t{n}"] = tiles(16, whole)
        shapes[f"back_t{n}"] = tiles(16, whole)
        shapes[f"final{n}"] = tiles(16, whole)
        shapes[f"landed{n}"] = tiles(16, whole)
        shapes[f"grad_s{n}"] = tiles(32, part)
        shapes[f"back_s{n}"] = tiles(32, part)
        for name, count in (
            ("bxs", 16), ("bxr", 16), ("bys", 32), ("byr", 32), ("bzs", 16), ("bzr", 16),
        ):
            shapes[f"{name}{n}"] = dma((count,))
    for name in ("qs", "ks", "vs", "gs", "qt", "kt", "vt", "gt"):
        shapes[name] = wide
    shapes.update(
        e_s=pltpu.VMEM(square, F32), d_s=pltpu.VMEM(square, F32),
        p_s=pltpu.VMEM(square, BF16), sl_s=pltpu.VMEM(square, BF16),
        e_t=pltpu.VMEM(small, F32), d_t=pltpu.VMEM(small, F32), p_t=pltpu.VMEM(small, BF16),
        stat_s=pltpu.VMEM((2, 8, ROWS), F32), scale_s=pltpu.VMEM((8, ROWS), F32),
        stat_t=pltpu.VMEM((2, 128, 128), F32),
    )
    for n in ("a", "b"):
        for name in ("to_s", "to_t", "from_s", "from_t"):
            shapes[name + n] = pltpu.VMEM((256, 128), F32)
        for name in ("tss", "tsr", "sts", "str"):
            shapes[name + n] = dma((32,))
    return shapes


def kernel(names, q_in, k_in, v_in, g_in, bias_ref, dq_out, dk_out, dv_out, *refs):
    m = dict(zip(names, refs, strict=True))
    tm = lax.axis_index("tm")
    tok = lax.axis_index("tok")
    x, zhi, core = lax.div(tm, 4), lax.rem(lax.div(tm, 2), 2), lax.rem(tm, 2)
    zlo, y = lax.div(tok, 4), lax.rem(tok, 4)
    z = zhi * 8 + zlo
    spot = x * 2 + core
    my_p = lax.rem(y, 2)
    my_pair = x * 8 + lax.div(y, 2) * 4 + core * 2 + my_p
    my_group = y * 8 + spot

    def remote(src, dst, s_sem, r_sem, target):
        return pltpu.make_async_remote_copy(
            src_ref=src, dst_ref=dst, send_sem=s_sem, recv_sem=r_sem,
            device_id=target, device_id_type=pl.DeviceIdType.MESH,
        )

    def start(src, dst, s_sem, r_sem, target, here):
        @pl.when(here)
        def _():
            pltpu.make_async_copy(src, dst, r_sem).start()

        @pl.when(jnp.logical_not(here))
        def _():
            remote(src, dst, s_sem, r_sem, target).start()

    def arrived(ref, sem):
        pltpu.make_async_copy(ref, ref, sem).wait()

    def sent(ref, sem, here):
        @pl.when(jnp.logical_not(here))
        def _():
            pltpu.make_async_copy(ref, ref, sem).wait()

    def loop(low, high, step):
        def one(n, _):
            step(n)
            return 0

        lax.fori_loop(low, high, one, 0)

    barrier = pltpu.get_barrier_semaphore()

    def hail(target):
        pl.semaphore_signal(
            barrier, inc=1, device_id=target, device_id_type=pl.DeviceIdType.MESH
        )

    loop(1, 16, lambda n: hail(device(x, lax.rem(z + far_step(n), 16), core, y)))

    def hail_plane(n):
        other = lax.rem(my_group + n, 32)
        there = lax.rem(other, 8)
        hail(device(lax.div(there, 2), z, lax.rem(there, 2), lax.div(other, 8)))

    loop(1, 32, hail_plane)

    def send_line(c):
        send, plane = m[f"send{c}"], m[f"plane{c}"]

        def one(n):
            to = lax.rem(z + far_step(n), 16)
            start(
                send.at[to], plane.at[z], m[f"zs{c}"].at[to], m[f"zr{c}"].at[z],
                device(x, to, core, y), to == z,
            )

        loop(1, 17, one)

    pack_first(q_in, k_in, m["send1"])
    pl.semaphore_wait(barrier, 46)
    send_line(1)
    pack_second(g_in, v_in, m["send2"], m["send3"])
    send_line(2)
    send_line(3)

    def forward(c, shift, part):
        plane, temp, spat = m[f"plane{c}"], m[f"temp{c}"], m[f"spat{c}"]

        def one(n):
            source = lax.rem(z + 16 - far_step(n), 16)
            hi, lo = lax.div(source, 8), lax.rem(source, 8)
            arrived(plane.at[source], m[f"zr{c}"].at[source])
            to_x, to_core = lax.div(lo, 2), lax.rem(lo, 2)
            slot = 4 * x + 2 * hi + core
            start(
                plane.at[source], temp.at[slot], m[f"xs{c}"].at[source], m[f"xr{c}"].at[slot],
                device(to_x, z, to_core, y), lo == spot,
            )
            for p in range(2):
                to_y = 2 * hi + p
                start(
                    plane.at[source, pl.ds(shift * p, part)], spat.at[y * 8 + lo],
                    m[f"ys{c}"].at[2 * source + p], m[f"yr{c}"].at[y * 8 + lo],
                    device(x, z, core, to_y), to_y == y,
                )

        loop(1, 17, one)

    def wait_x(c):
        loop(0, 16, lambda n: arrived(m[f"temp{c}"].at[n], m[f"xr{c}"].at[n]))

    def wait_y(c):
        loop(0, 32, lambda n: arrived(m[f"spat{c}"].at[n], m[f"yr{c}"].at[n]))

    def temp_tile(c, shift):
        return lambda i, t: m[f"temp{c}"][lax.div(i, 2), t + shift * lax.rem(i, 2)]

    def spat_tile(c):
        return lambda i, t: m[f"spat{c}"][i, t]

    def temp_pair(i):
        return lax.rem(i, 2)

    def spat_pair(i):
        return my_p

    def send_ts(c):
        to_s, from_t = m["to_s" + c], m["from_t" + c]
        turned = m["stat_t"][0 if c == "a" else 1].T
        to_s[...] = jnp.zeros_like(to_s)
        for j in range(2):
            to_s[pl.ds(j, 32, stride=8), :] = turned[32 * j : 32 * j + 32]

        def one(n):
            r = lax.rem(my_pair + n, 32)
            to_y = 2 * lax.rem(lax.div(r, 4), 2) + lax.rem(r, 2)
            start(
                to_s.at[pl.ds(pl.multiple_of(r * 8, 8), 8)],
                from_t.at[pl.ds(pl.multiple_of(my_group * 8, 8), 8)],
                m["tss" + c].at[r], m["tsr" + c].at[my_group],
                device(lax.div(r, 8), z, lax.rem(lax.div(r, 2), 2), to_y), r == my_pair,
            )

        loop(0, 32, one)

    def send_st(c):
        to_t, from_s = m["to_t" + c], m["from_s" + c]
        stat = m["stat_s"][0 if c == "a" else 1]
        row = lax.broadcasted_iota(jnp.int32, (256, ROWS), 0)
        lane = lax.broadcasted_iota(jnp.int32, (256, ROWS), 1)
        own = lax.div(lane, TOKENS) == lax.div(row, 8)
        spread = jnp.where(own, jnp.concatenate([stat] * 32, axis=0), 0.0)
        row = lax.broadcasted_iota(jnp.int32, (ROWS, 128), 0)
        lane = lax.broadcasted_iota(jnp.int32, (ROWS, 128), 1)
        pick = (lax.rem(row, TOKENS) == lane).astype(F32)
        to_t[...] = jnp.dot(spread, pick, precision=HIGHEST, preferred_element_type=F32)

        def one(n):
            i = lax.rem(my_group + n, 32)
            lo = lax.rem(i, 8)
            start(
                to_t.at[pl.ds(pl.multiple_of(i * 8, 8), 8)],
                from_s.at[pl.ds(pl.multiple_of(my_pair * 8, 8), 8)],
                m["sts" + c].at[i], m["str" + c].at[my_pair],
                device(lax.div(lo, 2), z, lax.rem(lo, 2), lax.div(i, 8)), i == my_group,
            )

        loop(0, 32, one)

    def got_s(c, count):
        from_s = m["from_s" + c]

        def one(n):
            arrived(from_s.at[pl.ds(pl.multiple_of(n * 8, 8), 8)], m["str" + c].at[n])

        loop(0, 32, one)
        return [
            jnp.concatenate(
                [from_s[pl.ds(2 * n + j, 32, stride=8), :] for j in range(2)], axis=0
            ).T[0:TOKENS]
            for n in range(count)
        ]

    def got_t(c, count):
        from_t = m["from_t" + c]

        def one(n):
            arrived(from_t.at[pl.ds(pl.multiple_of(n * 8, 8), 8)], m["tsr" + c].at[n])

        loop(0, 32, one)
        lane = lax.broadcasted_iota(jnp.int32, (64, ROWS), 1)
        row = lax.broadcasted_iota(jnp.int32, (64, ROWS), 0)
        own = lax.div(lane, TOKENS) == lax.rem(row, 32)
        got = jnp.concatenate([from_t[pl.ds(j, 32, stride=8), :] for j in range(2)], axis=0)
        lane = lax.broadcasted_iota(jnp.int32, (128, ROWS), 1)
        row = lax.broadcasted_iota(jnp.int32, (128, ROWS), 0)
        found = []
        for n in range(count):
            repeat = (lax.rem(lane, TOKENS) == row - TOKENS * n).astype(F32)
            wide = jnp.dot(got, repeat, precision=HIGHEST, preferred_element_type=F32)
            wide = jnp.where(own, wide, 0.0)
            found.append(
                jnp.concatenate(
                    [jnp.sum(wide[32 * j : 32 * j + 32], axis=0, keepdims=True) for j in range(2)],
                    axis=0,
                )
            )
        return found

    def scales(m1, l1, m2, l2):
        top = jnp.maximum(m1, m2)
        a1, a2 = jnp.exp(m1 - top), jnp.exp(m2 - top)
        mass = l1 * a1 + l2 * a2
        return a1 / mass, a2 / mass

    def return_x(c):
        grad, back = m["grad_t" + c], m["back_t" + c]

        def one(n):
            hi, there = lax.rem(n, 2), lax.rem(spot + lax.div(n, 2), 8)
            to_x, to_core = lax.div(there, 2), lax.rem(there, 2)
            source = hi * 8 + spot
            start(
                grad.at[4 * to_x + 2 * hi + to_core], back.at[source],
                m["bxs" + c].at[hi * 8 + there], m["bxr" + c].at[source],
                device(to_x, z, to_core, y), there == spot,
            )

        loop(0, 16, one)

    def return_y(c):
        grad, back = m["grad_s" + c], m["back_s" + c]

        def one(n):
            lo = lax.rem(zlo + far_step(lax.div(n, 4) + 1), 8)
            to_y = lax.rem(y + lax.rem(n, 4), 4)
            start(
                grad.at[to_y * 8 + lo], back.at[y * 8 + lo],
                m["bys" + c].at[to_y * 8 + lo], m["byr" + c].at[y * 8 + lo],
                device(x, z, core, to_y), to_y == y,
            )

        loop(0, 32, one)

    def go_home(c, whole, shift, part):
        back_s, back_t, final = m["back_s" + c], m["back_t" + c], m["final" + c]

        def one(n):
            to = lax.rem(z + far_step(n), 16)
            hi, lo = lax.div(to, 8), lax.rem(to, 8)
            arrived(back_t.at[to], m["bxr" + c].at[to])
            for p in range(2):
                slot = (2 * hi + p) * 8 + lo
                arrived(back_s.at[slot], m["byr" + c].at[slot])
            for t in range(whole):
                total = back_t[to, t].astype(F32)
                for p in range(2):
                    if 0 <= t - shift * p < part:
                        total = total + back_s[(2 * hi + p) * 8 + lo, t - shift * p].astype(F32)
                final[to, t] = total.astype(BF16)
            start(
                final.at[to], m["landed" + c].at[z], m["bzs" + c].at[to], m["bzr" + c].at[z],
                device(x, to, core, y), to == z,
            )

        loop(1, 17, one)

    def wait_home(c):
        loop(0, 16, lambda n: arrived(m["landed" + c].at[n], m["bzr" + c].at[n]))

    def drain(c):
        def one(n):
            hi, lo = lax.div(n, 8), lax.rem(n, 8)
            sent(m[f"send{c}"].at[n], m[f"zs{c}"].at[n], n == z)
            sent(m[f"plane{c}"].at[n], m[f"xs{c}"].at[n], lo == spot)
            for p in range(2):
                sent(m[f"spat{c}"].at[n], m[f"ys{c}"].at[2 * n + p], 2 * hi + p == y)

        loop(0, 16, one)

    def drain_back(c):
        def one(n):
            sent(m["final" + c].at[n], m["bzs" + c].at[n], n == z)
            sent(m["grad_t" + c].at[n], m["bxs" + c].at[n], lax.rem(n, 8) == spot)

        loop(0, 16, one)
        loop(
            0, 32,
            lambda n: sent(m["grad_s" + c].at[n], m["bys" + c].at[n], lax.div(n, 8) == y),
        )

    def drain_stats(c):
        def one(n):
            at = pl.ds(pl.multiple_of(n * 8, 8), 8)
            sent(m["to_s" + c].at[at], m["tss" + c].at[n], n == my_pair)
            sent(m["to_t" + c].at[at], m["sts" + c].at[n], n == my_group)

        loop(0, 32, one)

    qs, ks, vs, gs = m["qs"], m["ks"], m["vs"], m["gs"]
    qt, kt, vt, gt = m["qt"], m["kt"], m["vt"], m["gt"]
    e_s, d_s, p_s, sl_s = m["e_s"], m["d_s"], m["p_s"], m["sl_s"]
    e_t, d_t, p_t = m["e_t"], m["d_t"], m["p_t"]
    stat_s, stat_t, scale_s = m["stat_s"], m["stat_t"], m["scale_s"]
    stat_s[...] = jnp.zeros_like(stat_s)
    stat_t[...] = jnp.zeros_like(stat_t)

    forward(1, 3, 4)
    wait_x(1)
    unpack_first(temp_tile(1, 3), temp_pair, qt, kt)
    frame_k = lax.broadcasted_iota(jnp.int32, (64, 64), 0)
    frame_q = lax.broadcasted_iota(jnp.int32, (64, 64), 1)
    frame_k = 2 * lax.rem(frame_k, 32) + lax.div(frame_k, 32)
    frame_q = 2 * lax.rem(frame_q, 32) + lax.div(frame_q, 32)
    bias = jnp.full((64, 64), -jnp.inf, F32)
    for j in range(2 * BAND):
        o = j - BAND if j < BAND else j - BAND + 1
        bias = jnp.where(frame_k - frame_q == o, bias_ref[z, j], bias)
    for t in range(TOKENS):
        at = pl.ds(t, 64, stride=TOKENS)
        s = lax.dot_general(
            kt[at, :].astype(BF16), qt[at, :].astype(BF16), NT, preferred_element_type=F32
        ) * SCALE + bias
        top = jnp.max(s, axis=0, keepdims=True)
        e = jnp.exp(s - top)
        e_t[t] = e
        stat_t[0, t : t + 1, 0:64] = top
        stat_t[0, 24 + t : 25 + t, 0:64] = jnp.sum(e, axis=0, keepdims=True)
    send_ts("a")

    wait_y(1)
    unpack_first(spat_tile(1), spat_pair, qs, ks)

    def tile_at(n):
        j, b = lax.div(n, 3), lax.rem(n, 3)
        return (
            j,
            pl.ds(pl.multiple_of(j * ROWS, 8), ROWS),
            pl.ds(pl.multiple_of(j * ROWS + b * 256, 8), 256),
            pl.ds(pl.multiple_of(b * 256, 128), 256),
        )

    def scores(n):
        j, keys_at, rows_at, lanes_at = tile_at(n)
        s = lax.dot_general(
            ks[keys_at, :].astype(BF16), qs[rows_at, :].astype(BF16), NT,
            preferred_element_type=F32,
        ) * SCALE
        top = jnp.max(s, axis=0, keepdims=True)
        e = jnp.exp(s - top)
        e_s[j, :, lanes_at] = e
        stat_s[0, pl.ds(j, 1), lanes_at] = top
        stat_s[0, pl.ds(2 + j, 1), lanes_at] = jnp.sum(e, axis=0, keepdims=True)

    loop(0, 6, scores)
    send_st("a")

    forward(2, 1, 3)
    scale_t, other_t = scales(
        stat_t[0, 0:24, 0:64], stat_t[0, 24:48, 0:64], *got_s("a", 2)
    )
    wait_x(2)
    unpack_second(temp_tile(2, 1), temp_pair, gt)
    for t in range(TOKENS):
        at = pl.ds(t, 64, stride=TOKENS)
        rounded = (e_t[t] * scale_t[t : t + 1]).astype(BF16)
        p_t[t] = rounded
        vt[at, :] = jnp.dot(rounded, gt[at, :].astype(BF16), preferred_element_type=F32)

    def pack_values_t(n):
        own0, shared0, extra0 = value_tiles(load_rows(vt, 2 * n), 0)
        own1, shared1, extra1 = value_tiles(load_rows(vt, 2 * n + 1), 1)
        out = m["grad_tv"]
        out[n, 0] = own0.astype(BF16)
        out[n, 1] = (shared0 + shared1).astype(BF16)
        out[n, 2] = (extra0 + extra1).astype(BF16)
        out[n, 3] = own1.astype(BF16)

    loop(0, 16, pack_values_t)
    return_x("v")

    scale_own, scale_other = scales(stat_s[0, 0:2], stat_s[0, 2:4], *got_t("a", 2))
    scale_s[0:2] = scale_own
    scale_s[2:4] = scale_other

    def weights(n):
        j, _, _, lanes_at = tile_at(n)
        p_s[j, :, lanes_at] = (e_s[j, :, lanes_at] * scale_s[pl.ds(j, 1), lanes_at]).astype(BF16)

    loop(0, 6, weights)
    wait_y(2)
    unpack_second(spat_tile(2), spat_pair, gs)

    def value_grads(j):
        rows_at = pl.ds(pl.multiple_of(j * ROWS, 8), ROWS)
        vs[rows_at, :] = jnp.dot(
            p_s[j], gs[rows_at, :].astype(BF16), preferred_element_type=F32
        )

    loop(0, 2, value_grads)

    def pack_values_s(i):
        own, shared, extra = value_tiles(load_rows(vs, i), my_p)
        out = m["grad_sv"]
        out[i, 2 * my_p] = own.astype(BF16)
        out[i, 1 - my_p] = shared.astype(BF16)
        out[i, 2 - my_p] = extra.astype(BF16)

    loop(0, 32, pack_values_s)
    return_y("v")
    forward(3, 1, 2)
    go_home("v", 4, 1, 3)

    wait_x(3)
    unpack_third(temp_tile(3, 1), temp_tile(2, 1), temp_pair, vt)
    for t in range(TOKENS):
        at = pl.ds(t, 64, stride=TOKENS)
        d = lax.dot_general(
            vt[at, :].astype(BF16), gt[at, :].astype(BF16), NT, preferred_element_type=F32
        )
        d_t[t] = d
        stat_t[1, t : t + 1, 0:64] = jnp.sum(e_t[t] * d, axis=0, keepdims=True)
    send_ts("b")
    wait_y(3)
    unpack_third(spat_tile(3), spat_tile(2), spat_pair, vs)

    def dots(n):
        j, keys_at, rows_at, lanes_at = tile_at(n)
        d = lax.dot_general(
            vs[keys_at, :].astype(BF16), gs[rows_at, :].astype(BF16), NT,
            preferred_element_type=F32,
        )
        d_s[j, :, lanes_at] = d
        stat_s[1, pl.ds(j, 1), lanes_at] = jnp.sum(e_s[j, :, lanes_at] * d, axis=0, keepdims=True)

    loop(0, 6, dots)
    send_st("b")

    (moment_s,) = got_s("b", 1)
    delta_t = stat_t[1, 0:24, 0:64] * scale_t + moment_s * other_t
    for t in range(TOKENS):
        at = pl.ds(t, 64, stride=TOKENS)
        slope = (p_t[t].astype(F32) * (d_t[t] - delta_t[t : t + 1])).astype(BF16)
        k = kt[at, :].astype(BF16)
        q = qt[at, :].astype(BF16)
        kt[at, :] = jnp.dot(slope, q, preferred_element_type=F32) * SCALE
        across = slope.astype(F32).T.astype(BF16)
        qt[at, :] = jnp.dot(across, k, preferred_element_type=F32) * SCALE

    def pack_keys_t(n):
        main0, extra0 = key_tiles(load_rows(qt, 2 * n), load_rows(kt, 2 * n), 0)
        main1, extra1 = key_tiles(load_rows(qt, 2 * n + 1), load_rows(kt, 2 * n + 1), 1)
        out = m["grad_tk"]
        for r in range(3):
            out[n, r] = main0[r].astype(BF16)
            out[n, 4 + r] = main1[r].astype(BF16)
        out[n, 3] = (extra0 + extra1).astype(BF16)

    loop(0, 16, pack_keys_t)
    return_x("k")

    (moment_t,) = got_t("b", 1)
    scale_s[4:6] = stat_s[1, 0:2] * scale_s[0:2] + moment_t * scale_s[2:4]

    def slopes(n):
        j, _, _, lanes_at = tile_at(n)
        gap = d_s[j, :, lanes_at] - scale_s[pl.ds(4 + j, 1), lanes_at]
        sl_s[j, :, lanes_at] = (p_s[j, :, lanes_at].astype(F32) * gap).astype(BF16)

    loop(0, 6, slopes)

    def key_grads(j):
        rows_at = pl.ds(pl.multiple_of(j * ROWS, 8), ROWS)
        q = qs[rows_at, :].astype(BF16)
        k_turned = ks[rows_at, :].T.astype(BF16)
        ks[rows_at, :] = jnp.dot(sl_s[j], q, preferred_element_type=F32) * SCALE
        qs[rows_at, :] = jnp.dot(k_turned, sl_s[j], preferred_element_type=F32).T * SCALE

    loop(0, 2, key_grads)

    def pack_keys_s(i):
        main, extra = key_tiles(load_rows(qs, i), load_rows(ks, i), my_p)
        out = m["grad_sk"]
        for r in range(3):
            out[i, r + my_p] = main[r].astype(BF16)
        out[i, 3 - 3 * my_p] = extra.astype(BF16)

    loop(0, 32, pack_keys_s)
    return_y("k")
    go_home("k", 7, 3, 4)

    wait_home("v")
    restore_values(m["landedv"], dv_out)
    for c in (1, 2, 3):
        drain(c)
    for c in ("a", "b"):
        drain_stats(c)
    drain_back("v")
    wait_home("k")
    restore_keys(m["landedk"], dq_out, dk_out)
    drain_back("k")


def body(queries, keys, values, out_grad, time_bias):
    vmem = pl.BlockSpec(memory_space=pltpu.VMEM)
    shape = jax.ShapeDtypeStruct(queries.shape, BF16)
    shapes = scratch()

    def run(*refs):
        kernel(list(shapes), *refs)

    return pl.pallas_call(
        run,
        out_shape=(shape, shape, shape),
        in_specs=[vmem] * 4 + [pl.BlockSpec(memory_space=pltpu.SMEM)],
        out_specs=(vmem, vmem, vmem),
        scratch_shapes=list(shapes.values()),
        compiler_params=pltpu.CompilerParams(
            collective_id=0, has_side_effects=True, vmem_limit_bytes=56 * 2**20
        ),
    )(queries, keys, values, out_grad, time_bias)


def solution(mesh):
    spec = P("tm", "tok", None)
    return jax.shard_map(
        body, mesh=mesh, in_specs=(spec, spec, spec, spec, P()),
        out_specs=(spec, spec, spec), check_vma=False,
    )
```

```python
import jax
import jax.numpy as jnp
from jax import lax
from jax.experimental import pallas as pl
from jax.experimental.pallas import tpu as pltpu
from jax.sharding import PartitionSpec as P

F32 = jnp.float32
BF16 = jnp.bfloat16
HEADS = 16
DIM = 72
TOKENS = 24
WIDTH = HEADS * DIM
BAND = 8
GROUPS = 32
ROWS = GROUPS * TOKENS
PAIR = 2 * TOKENS
SCALE = DIM**-0.5
NT = (((1,), (1,)), ((), ()))
HIGHEST = lax.Precision.HIGHEST


def device(x, z, core, y):
    return (x * 4 + lax.div(z, 8) * 2 + core, lax.rem(z, 8) * 4 + y)


def lanes_of(rows):
    return lax.broadcasted_iota(jnp.int32, (rows, 128), 1)


def turn(value, shift):
    if isinstance(shift, int):
        shift %= 128
        return value if shift == 0 else pltpu.roll(value, shift, 1)
    return pltpu.roll(value, lax.rem(shift + 256, 128), 1)


def group(value, r):
    return value[16 * r : 16 * r + 16]


def head_run(ref, pair, head):
    first, offset = head * DIM // 128, head * DIM % 128
    tile = [
        jnp.concatenate(
            [ref[2 * pair + j, :, 128 * t : 128 * t + 128].astype(F32) for j in range(2)], axis=0
        )
        for t in range(first, first + (2 if offset + DIM > 128 else 1))
    ]
    if len(tile) == 1:
        return tile[0], offset
    return jnp.where(lanes_of(PAIR) >= offset, tile[0], tile[1]), offset


def pack_first(q_in, k_in, out):
    lane, lane16 = lanes_of(PAIR), lanes_of(16)
    for head in range(HEADS):
        extra = None
        for pair in range(2):
            q, at = head_run(q_in, pair, head)
            k, _ = head_run(k_in, pair, head)
            k = turn(k, 72 - at)
            main = jnp.where(lane < DIM, turn(q, -at), k).astype(BF16)
            for r in range(3):
                out[head, 4 * pair + r] = group(main, r)
                low = 16 * (3 * pair + r)
                piece = turn(group(k, r), low)
                extra = piece if extra is None else jnp.where(lane16 >= low, piece, extra)
        out[head, 3] = extra.astype(BF16)


def pack_second(g_in, v_in, out_g, out_v):
    lane16 = lanes_of(16)
    half = lane16 < 64
    for head in range(HEADS):
        extra = None
        shared_g, shared_v = [], []
        for pair in range(2):
            g, at = head_run(g_in, pair, head)
            v, _ = head_run(v_in, pair, head)
            g = turn(g, -at)
            v = turn(v, -at - 8)
            out_g[head, 3 * pair] = jnp.where(half, group(g, 0), turn(group(g, 1), 64)).astype(BF16)
            out_v[head, 2 * pair] = jnp.where(half, group(v, 0), turn(group(v, 1), 64)).astype(BF16)
            shared_g.append(group(g, 2))
            shared_v.append(group(v, 2))
            for r in range(3):
                low = 16 * (3 * pair + r)
                piece = turn(group(g, r), low - 64)
                extra = piece if extra is None else jnp.where(lane16 >= low, piece, extra)
                extra = jnp.where(lane16 >= low + 8, turn(group(v, r), low + 16), extra)
        out_g[head, 1] = jnp.where(half, shared_g[0], turn(shared_g[1], 64)).astype(BF16)
        out_v[head, 1] = jnp.where(half, shared_v[0], turn(shared_v[1], 64)).astype(BF16)
        out_g[head, 2] = extra.astype(BF16)


def open_first(plane, wide, source):
    lane = lanes_of(16)
    extra = plane[source, 3].astype(F32)
    for p in range(2):
        for r in range(3):
            main = plane[source, 4 * p + r].astype(F32)
            k = jnp.where(lane >= DIM, main, turn(extra, -48 * p - 16 * r))
            wide[source, p, r] = jnp.where(lane < DIM, main, 0.0).astype(BF16)
            wide[source, p, 3 + r] = turn(k, 56).astype(BF16)


def open_second(plane, wide, source):
    lane = lanes_of(16)
    shared = plane[source, 1].astype(F32)
    extra = plane[source, 2].astype(F32)
    for p in range(2):
        own = plane[source, 3 * p].astype(F32)
        for r, main in enumerate((own, turn(own, 64), turn(shared, 64 * p))):
            tail = jnp.where(lane < DIM, turn(extra, 64 - 48 * p - 16 * r), 0.0)
            wide[source, p, r] = jnp.where(lane < 64, main, tail).astype(BF16)


def open_third(plane, plane_g, wide, source):
    lane = lanes_of(16)
    shared = plane[source, 1].astype(F32)
    extra = plane_g[source, 2].astype(F32)
    for p in range(2):
        own = plane[source, 2 * p].astype(F32)
        for r, main in enumerate((turn(own, 8), turn(own, 72), turn(shared, 8 - 64 * p))):
            head = turn(extra, -8 - 48 * p - 16 * r)
            wide[source, p, r] = jnp.where(lane < 8, head, main).astype(BF16)


def gather_rows(tiles, first, ref):
    def one(i, _):
        value = jnp.concatenate([tiles[i, first + r].astype(F32) for r in range(3)], axis=0)
        for j in range(2):
            at = pl.ds(pl.multiple_of(j * ROWS + i * TOKENS, 8), TOKENS)
            ref[at, :] = value[j * TOKENS : (j + 1) * TOKENS]
        return 0

    lax.fori_loop(0, GROUPS, one, 0, unroll=8)


def scatter_rows(ref, tiles, first):
    def one(i, _):
        value = jnp.concatenate(
            [
                ref[pl.ds(pl.multiple_of(j * ROWS + i * TOKENS, 8), TOKENS), :]
                for j in range(2)
            ],
            axis=0,
        )
        for r in range(3):
            tiles[i, first + r] = group(value, r).astype(BF16)
        return 0

    lax.fori_loop(0, GROUPS, one, 0, unroll=8)


def close_values(dv, out, to):
    lane = lanes_of(16)
    half = lane < 64
    for p in range(2):
        out[to, 3 * p] = jnp.where(half, dv[p][0], turn(dv[p][1], 64)).astype(BF16)
    out[to, 1] = jnp.where(half, dv[0][2], turn(dv[1][2], 64)).astype(BF16)
    extra = None
    for p in range(2):
        for r in range(3):
            low = 16 * (3 * p + r)
            piece = turn(dv[p][r], low - 64)
            extra = piece if extra is None else jnp.where(lane >= low, piece, extra)
    out[to, 2] = extra.astype(BF16)


def close_keys(dq, dk, out, to):
    lane = lanes_of(16)
    extra = None
    for p in range(2):
        for r in range(3):
            low = 16 * (3 * p + r)
            k = turn(dk[p][r], 72)
            out[to, 4 * p + r] = jnp.where(lane < DIM, dq[p][r], k).astype(BF16)
            piece = turn(k, low)
            extra = piece if extra is None else jnp.where(lane >= low, piece, extra)
    out[to, 3] = extra.astype(BF16)


def spread_heads(parts, out, pair):
    lane = lanes_of(PAIR)
    for t in range(WIDTH // 128):
        whole = None
        for head in reversed(range(HEADS)):
            low, high = head * DIM - 128 * t, head * DIM + DIM - 128 * t
            if high <= 0 or low >= 128:
                continue
            whole = parts[head] if whole is None else jnp.where(lane < high, parts[head], whole)
        for j in range(2):
            out[2 * pair + j, :, 128 * t : 128 * t + 128] = whole[
                TOKENS * j : TOKENS * j + TOKENS
            ].astype(BF16)


def restore_values(landed, dv_out):
    for pair in range(2):
        parts = []
        lane = lanes_of(PAIR)
        for head in range(HEADS):
            own = landed[head, 3 * pair].astype(F32)
            shared = landed[head, 1].astype(F32)
            extra = landed[head, 2].astype(F32)
            main = jnp.concatenate([own, turn(own, 64), turn(shared, 64 * pair)], axis=0)
            tail = jnp.concatenate(
                [turn(extra, 64 - 48 * pair - 16 * r) for r in range(3)], axis=0
            )
            parts.append(turn(jnp.where(lane < 64, main, tail), head * DIM))
        spread_heads(parts, dv_out, pair)


def restore_keys(landed, dq_out, dk_out):
    for pair in range(2):
        lane = lanes_of(PAIR)
        q_parts, k_parts = [], []
        for head in range(HEADS):
            main = jnp.concatenate(
                [landed[head, 4 * pair + r].astype(F32) for r in range(3)], axis=0
            )
            extra = landed[head, 3].astype(F32)
            extra = jnp.concatenate([turn(extra, -48 * pair - 16 * r) for r in range(3)], axis=0)
            q_parts.append(turn(main, head * DIM))
            k_parts.append(turn(jnp.where(lane >= DIM, main, extra), head * DIM - DIM))
        spread_heads(q_parts, dq_out, pair)
        spread_heads(k_parts, dk_out, pair)


def far_step(n):
    return jnp.where(lax.rem(n, 2) == 1, 8 + lax.div(n, 2), 8 - lax.div(n, 2))


def scratch():
    dma = pltpu.SemaphoreType.DMA

    def tiles(blocks, count):
        return pltpu.VMEM((blocks, count, 16, 128), BF16)

    wide = pltpu.VMEM((2 * ROWS, 128), F32)
    square = (2, ROWS, ROWS)
    small = (TOKENS, 64, 64)
    shapes = {}
    for n, (whole, part) in {1: (7, 6), 2: (4, 3), 3: (3, 3)}.items():
        shapes[f"send{n}"] = tiles(16, whole)
        shapes[f"plane{n}"] = tiles(16, whole)
        shapes[f"wide{n}"] = pltpu.VMEM((16, 2, part, 16, 128), BF16)
        shapes[f"temp{n}"] = tiles(32, part)
        shapes[f"spat{n}"] = tiles(32, part)
        for name, count in (("zs", 16), ("zr", 16), ("xs", 16), ("xr", 16), ("ys", 32), ("yr", 32)):
            shapes[f"{name}{n}"] = dma((count,))
    for n, (whole, part) in {"v": (4, 3), "k": (7, 6)}.items():
        shapes[f"grad_t{n}"] = tiles(32, part)
        shapes[f"back_t{n}"] = pltpu.VMEM((16, 2, part, 16, 128), BF16)
        shapes[f"final{n}"] = tiles(16, whole)
        shapes[f"landed{n}"] = tiles(16, whole)
        shapes[f"grad_s{n}"] = tiles(32, part)
        shapes[f"back_s{n}"] = tiles(32, part)
        for name, count in (
            ("bxs", 16), ("bxr", 16), ("bys", 32), ("byr", 32), ("bzs", 16), ("bzr", 16),
        ):
            shapes[f"{name}{n}"] = dma((count,))
    for name in ("qs", "ks", "vs", "gs", "qt", "kt", "vt", "gt"):
        shapes[name] = wide
    shapes.update(
        e_s=pltpu.VMEM(square, F32), d_s=pltpu.VMEM(square, F32),
        p_s=pltpu.VMEM(square, BF16), sl_s=pltpu.VMEM(square, BF16),
        e_t=pltpu.VMEM(small, F32), d_t=pltpu.VMEM(small, F32), p_t=pltpu.VMEM(small, BF16),
        stat_s=pltpu.VMEM((2, 8, ROWS), F32), scale_s=pltpu.VMEM((8, ROWS), F32),
        stat_t=pltpu.VMEM((2, 128, 128), F32),
    )
    for n in ("a", "b"):
        for name in ("to_s", "to_t", "from_s", "from_t"):
            shapes[name + n] = pltpu.VMEM((256, 128), F32)
        for name in ("tss", "tsr", "sts", "str"):
            shapes[name + n] = dma((32,))
    return shapes


def kernel(names, q_in, k_in, v_in, g_in, bias_ref, dq_out, dk_out, dv_out, *refs):
    m = dict(zip(names, refs, strict=True))
    tm = lax.axis_index("tm")
    tok = lax.axis_index("tok")
    x, zhi, core = lax.div(tm, 4), lax.rem(lax.div(tm, 2), 2), lax.rem(tm, 2)
    zlo, y = lax.div(tok, 4), lax.rem(tok, 4)
    z = zhi * 8 + zlo
    spot = x * 2 + core
    my_p = lax.rem(y, 2)
    my_pair = x * 8 + lax.div(y, 2) * 4 + core * 2 + my_p
    my_group = y * 8 + spot

    def remote(src, dst, s_sem, r_sem, target):
        return pltpu.make_async_remote_copy(
            src_ref=src, dst_ref=dst, send_sem=s_sem, recv_sem=r_sem,
            device_id=target, device_id_type=pl.DeviceIdType.MESH,
        )

    def start(src, dst, s_sem, r_sem, target, here):
        @pl.when(here)
        def _():
            pltpu.make_async_copy(src, dst, r_sem).start()

        @pl.when(jnp.logical_not(here))
        def _():
            remote(src, dst, s_sem, r_sem, target).start()

    def arrived(ref, sem):
        pltpu.make_async_copy(ref, ref, sem).wait()

    def sent(ref, sem, here):
        @pl.when(jnp.logical_not(here))
        def _():
            pltpu.make_async_copy(ref, ref, sem).wait()

    def loop(low, high, step):
        def one(n, _):
            step(n)
            return 0

        lax.fori_loop(low, high, one, 0)

    barrier = pltpu.get_barrier_semaphore()

    def hail(target):
        pl.semaphore_signal(
            barrier, inc=1, device_id=target, device_id_type=pl.DeviceIdType.MESH
        )

    loop(1, 16, lambda n: hail(device(x, lax.rem(z + far_step(n), 16), core, y)))

    def hail_plane(n):
        other = lax.rem(my_group + n, 32)
        there = lax.rem(other, 8)
        hail(device(lax.div(there, 2), z, lax.rem(there, 2), lax.div(other, 8)))

    loop(1, 32, hail_plane)

    def send_line(c):
        send, plane = m[f"send{c}"], m[f"plane{c}"]

        def one(n):
            to = lax.rem(z + far_step(n), 16)
            start(
                send.at[to], plane.at[z], m[f"zs{c}"].at[to], m[f"zr{c}"].at[z],
                device(x, to, core, y), to == z,
            )

        loop(1, 17, one)

    pack_first(q_in, k_in, m["send1"])
    pl.semaphore_wait(barrier, 46)
    send_line(1)
    pack_second(g_in, v_in, m["send2"], m["send3"])
    send_line(2)
    send_line(3)

    def forward(c, unpack):
        plane, wide, temp, spat = m[f"plane{c}"], m[f"wide{c}"], m[f"temp{c}"], m[f"spat{c}"]

        def one(n):
            source = lax.rem(z + 16 - far_step(n), 16)
            hi, lo = lax.div(source, 8), lax.rem(source, 8)
            arrived(plane.at[source], m[f"zr{c}"].at[source])
            unpack(source)
            to_x, to_core = lax.div(lo, 2), lax.rem(lo, 2)
            slot = 4 * x + 2 * hi + core
            start(
                wide.at[source], temp.at[pl.ds(pl.multiple_of(2 * slot, 2), 2)],
                m[f"xs{c}"].at[source], m[f"xr{c}"].at[slot],
                device(to_x, z, to_core, y), lo == spot,
            )
            for p in range(2):
                to_y = 2 * hi + p
                start(
                    wide.at[source, p], spat.at[y * 8 + lo],
                    m[f"ys{c}"].at[2 * source + p], m[f"yr{c}"].at[y * 8 + lo],
                    device(x, z, core, to_y), to_y == y,
                )

        loop(1, 17, one)

    def wait_x(c):
        def one(n):
            arrived(m[f"temp{c}"].at[pl.ds(pl.multiple_of(2 * n, 2), 2)], m[f"xr{c}"].at[n])

        loop(0, 16, one)

    def wait_y(c):
        loop(0, 32, lambda n: arrived(m[f"spat{c}"].at[n], m[f"yr{c}"].at[n]))

    def send_ts(c):
        to_s, from_t = m["to_s" + c], m["from_t" + c]
        turned = m["stat_t"][0 if c == "a" else 1].T
        to_s[...] = jnp.zeros_like(to_s)
        for j in range(2):
            to_s[pl.ds(j, 32, stride=8), :] = turned[32 * j : 32 * j + 32]

        def one(n):
            r = lax.rem(my_pair + n, 32)
            to_y = 2 * lax.rem(lax.div(r, 4), 2) + lax.rem(r, 2)
            start(
                to_s.at[pl.ds(pl.multiple_of(r * 8, 8), 8)],
                from_t.at[pl.ds(pl.multiple_of(my_group * 8, 8), 8)],
                m["tss" + c].at[r], m["tsr" + c].at[my_group],
                device(lax.div(r, 8), z, lax.rem(lax.div(r, 2), 2), to_y), r == my_pair,
            )

        loop(0, 32, one)

    def send_st(c):
        to_t, from_s = m["to_t" + c], m["from_s" + c]
        stat = m["stat_s"][0 if c == "a" else 1]
        row = lax.broadcasted_iota(jnp.int32, (256, ROWS), 0)
        lane = lax.broadcasted_iota(jnp.int32, (256, ROWS), 1)
        own = lax.div(lane, TOKENS) == lax.div(row, 8)
        spread = jnp.where(own, jnp.concatenate([stat] * 32, axis=0), 0.0)
        row = lax.broadcasted_iota(jnp.int32, (ROWS, 128), 0)
        lane = lax.broadcasted_iota(jnp.int32, (ROWS, 128), 1)
        pick = (lax.rem(row, TOKENS) == lane).astype(F32)
        to_t[...] = jnp.dot(spread, pick, precision=HIGHEST, preferred_element_type=F32)

        def one(n):
            i = lax.rem(my_group + n, 32)
            lo = lax.rem(i, 8)
            start(
                to_t.at[pl.ds(pl.multiple_of(i * 8, 8), 8)],
                from_s.at[pl.ds(pl.multiple_of(my_pair * 8, 8), 8)],
                m["sts" + c].at[i], m["str" + c].at[my_pair],
                device(lax.div(lo, 2), z, lax.rem(lo, 2), lax.div(i, 8)), i == my_group,
            )

        loop(0, 32, one)

    def got_s(c, count):
        from_s = m["from_s" + c]

        def one(n):
            arrived(from_s.at[pl.ds(pl.multiple_of(n * 8, 8), 8)], m["str" + c].at[n])

        loop(0, 32, one)
        return [
            jnp.concatenate(
                [from_s[pl.ds(2 * n + j, 32, stride=8), :] for j in range(2)], axis=0
            ).T[0:TOKENS]
            for n in range(count)
        ]

    def got_t(c, count):
        from_t = m["from_t" + c]

        def one(n):
            arrived(from_t.at[pl.ds(pl.multiple_of(n * 8, 8), 8)], m["tsr" + c].at[n])

        loop(0, 32, one)
        lane = lax.broadcasted_iota(jnp.int32, (64, ROWS), 1)
        row = lax.broadcasted_iota(jnp.int32, (64, ROWS), 0)
        own = lax.div(lane, TOKENS) == lax.rem(row, 32)
        got = jnp.concatenate([from_t[pl.ds(j, 32, stride=8), :] for j in range(2)], axis=0)
        lane = lax.broadcasted_iota(jnp.int32, (128, ROWS), 1)
        row = lax.broadcasted_iota(jnp.int32, (128, ROWS), 0)
        found = []
        for n in range(count):
            repeat = (lax.rem(lane, TOKENS) == row - TOKENS * n).astype(F32)
            wide = jnp.dot(got, repeat, precision=HIGHEST, preferred_element_type=F32)
            wide = jnp.where(own, wide, 0.0)
            found.append(
                jnp.concatenate(
                    [jnp.sum(wide[32 * j : 32 * j + 32], axis=0, keepdims=True) for j in range(2)],
                    axis=0,
                )
            )
        return found

    def scales(m1, l1, m2, l2):
        top = jnp.maximum(m1, m2)
        a1, a2 = jnp.exp(m1 - top), jnp.exp(m2 - top)
        mass = l1 * a1 + l2 * a2
        return a1 / mass, a2 / mass

    def return_x(c):
        grad, back = m["grad_t" + c], m["back_t" + c]

        def one(n):
            hi, there = lax.rem(n, 2), lax.rem(spot + lax.div(n, 2), 8)
            to_x, to_core = lax.div(there, 2), lax.rem(there, 2)
            source = hi * 8 + spot
            block = pl.ds(pl.multiple_of(2 * (4 * to_x + 2 * hi + to_core), 2), 2)
            start(
                grad.at[block], back.at[source],
                m["bxs" + c].at[hi * 8 + there], m["bxr" + c].at[source],
                device(to_x, z, to_core, y), there == spot,
            )

        loop(0, 16, one)

    def return_y(c):
        grad, back = m["grad_s" + c], m["back_s" + c]

        def one(n):
            lo = lax.rem(zlo + far_step(lax.div(n, 4) + 1), 8)
            to_y = lax.rem(y + lax.rem(n, 4), 4)
            start(
                grad.at[to_y * 8 + lo], back.at[y * 8 + lo],
                m["bys" + c].at[to_y * 8 + lo], m["byr" + c].at[y * 8 + lo],
                device(x, z, core, to_y), to_y == y,
            )

        loop(0, 32, one)

    def go_home(c, close):
        back_s, back_t, final = m["back_s" + c], m["back_t" + c], m["final" + c]

        def one(n):
            to = lax.rem(z + far_step(n), 16)
            hi, lo = lax.div(to, 8), lax.rem(to, 8)
            arrived(back_t.at[to], m["bxr" + c].at[to])
            for p in range(2):
                slot = (2 * hi + p) * 8 + lo
                arrived(back_s.at[slot], m["byr" + c].at[slot])

            def total(first):
                return [
                    [
                        back_t[to, p, first + r].astype(F32)
                        + back_s[(2 * hi + p) * 8 + lo, first + r].astype(F32)
                        for r in range(3)
                    ]
                    for p in range(2)
                ]

            close(total, final, to)
            start(
                final.at[to], m["landed" + c].at[z], m["bzs" + c].at[to], m["bzr" + c].at[z],
                device(x, to, core, y), to == z,
            )

        loop(1, 17, one)

    def wait_home(c):
        loop(0, 16, lambda n: arrived(m["landed" + c].at[n], m["bzr" + c].at[n]))

    def drain(c):
        def one(n):
            hi, lo = lax.div(n, 8), lax.rem(n, 8)
            sent(m[f"send{c}"].at[n], m[f"zs{c}"].at[n], n == z)
            sent(m[f"wide{c}"].at[n], m[f"xs{c}"].at[n], lo == spot)
            for p in range(2):
                sent(m[f"spat{c}"].at[n], m[f"ys{c}"].at[2 * n + p], 2 * hi + p == y)

        loop(0, 16, one)

    def drain_back(c):
        def one(n):
            sent(m["final" + c].at[n], m["bzs" + c].at[n], n == z)
            sent(m["back_t" + c].at[n], m["bxs" + c].at[n], lax.rem(n, 8) == spot)

        loop(0, 16, one)
        loop(
            0, 32,
            lambda n: sent(m["grad_s" + c].at[n], m["bys" + c].at[n], lax.div(n, 8) == y),
        )

    def drain_stats(c):
        def one(n):
            at = pl.ds(pl.multiple_of(n * 8, 8), 8)
            sent(m["to_s" + c].at[at], m["tss" + c].at[n], n == my_pair)
            sent(m["to_t" + c].at[at], m["sts" + c].at[n], n == my_group)

        loop(0, 32, one)

    qs, ks, vs, gs = m["qs"], m["ks"], m["vs"], m["gs"]
    qt, kt, vt, gt = m["qt"], m["kt"], m["vt"], m["gt"]
    e_s, d_s, p_s, sl_s = m["e_s"], m["d_s"], m["p_s"], m["sl_s"]
    e_t, d_t, p_t = m["e_t"], m["d_t"], m["p_t"]
    stat_s, stat_t, scale_s = m["stat_s"], m["stat_t"], m["scale_s"]
    stat_s[...] = jnp.zeros_like(stat_s)
    stat_t[...] = jnp.zeros_like(stat_t)

    forward(1, lambda source: open_first(m["plane1"], m["wide1"], source))
    wait_x(1)
    gather_rows(m["temp1"], 0, qt)
    gather_rows(m["temp1"], 3, kt)
    frame_k = lax.broadcasted_iota(jnp.int32, (64, 64), 0)
    frame_q = lax.broadcasted_iota(jnp.int32, (64, 64), 1)
    frame_k = 2 * lax.rem(frame_k, 32) + lax.div(frame_k, 32)
    frame_q = 2 * lax.rem(frame_q, 32) + lax.div(frame_q, 32)
    bias = jnp.full((64, 64), -jnp.inf, F32)
    for j in range(2 * BAND):
        o = j - BAND if j < BAND else j - BAND + 1
        bias = jnp.where(frame_k - frame_q == o, bias_ref[z, j], bias)
    for t in range(TOKENS):
        at = pl.ds(t, 64, stride=TOKENS)
        s = lax.dot_general(
            kt[at, :].astype(BF16), qt[at, :].astype(BF16), NT, preferred_element_type=F32
        ) * SCALE + bias
        top = jnp.max(s, axis=0, keepdims=True)
        e = jnp.exp(s - top)
        e_t[t] = e
        stat_t[0, t : t + 1, 0:64] = top
        stat_t[0, 24 + t : 25 + t, 0:64] = jnp.sum(e, axis=0, keepdims=True)
    send_ts("a")

    wait_y(1)
    gather_rows(m["spat1"], 0, qs)
    gather_rows(m["spat1"], 3, ks)

    def tile_at(n):
        j, b = lax.div(n, 3), lax.rem(n, 3)
        return (
            j,
            pl.ds(pl.multiple_of(j * ROWS, 8), ROWS),
            pl.ds(pl.multiple_of(j * ROWS + b * 256, 8), 256),
            pl.ds(pl.multiple_of(b * 256, 128), 256),
        )

    def scores(n):
        j, keys_at, rows_at, lanes_at = tile_at(n)
        s = lax.dot_general(
            ks[keys_at, :].astype(BF16), qs[rows_at, :].astype(BF16), NT,
            preferred_element_type=F32,
        ) * SCALE
        top = jnp.max(s, axis=0, keepdims=True)
        e = jnp.exp(s - top)
        e_s[j, :, lanes_at] = e
        stat_s[0, pl.ds(j, 1), lanes_at] = top
        stat_s[0, pl.ds(2 + j, 1), lanes_at] = jnp.sum(e, axis=0, keepdims=True)

    loop(0, 6, scores)
    send_st("a")

    forward(2, lambda source: open_second(m["plane2"], m["wide2"], source))
    scale_t, other_t = scales(
        stat_t[0, 0:24, 0:64], stat_t[0, 24:48, 0:64], *got_s("a", 2)
    )
    wait_x(2)
    gather_rows(m["temp2"], 0, gt)
    for t in range(TOKENS):
        at = pl.ds(t, 64, stride=TOKENS)
        rounded = (e_t[t] * scale_t[t : t + 1]).astype(BF16)
        p_t[t] = rounded
        vt[at, :] = jnp.dot(rounded, gt[at, :].astype(BF16), preferred_element_type=F32)

    scatter_rows(vt, m["grad_tv"], 0)
    return_x("v")

    scale_own, scale_other = scales(stat_s[0, 0:2], stat_s[0, 2:4], *got_t("a", 2))
    scale_s[0:2] = scale_own
    scale_s[2:4] = scale_other

    def weights(n):
        j, _, _, lanes_at = tile_at(n)
        p_s[j, :, lanes_at] = (e_s[j, :, lanes_at] * scale_s[pl.ds(j, 1), lanes_at]).astype(BF16)

    loop(0, 6, weights)
    wait_y(2)
    gather_rows(m["spat2"], 0, gs)

    def value_grads(j):
        rows_at = pl.ds(pl.multiple_of(j * ROWS, 8), ROWS)
        vs[rows_at, :] = jnp.dot(
            p_s[j], gs[rows_at, :].astype(BF16), preferred_element_type=F32
        )

    loop(0, 2, value_grads)

    scatter_rows(vs, m["grad_sv"], 0)
    return_y("v")
    forward(3, lambda source: open_third(m["plane3"], m["plane2"], m["wide3"], source))
    go_home("v", lambda total, out, to: close_values(total(0), out, to))

    wait_x(3)
    gather_rows(m["temp3"], 0, vt)
    for t in range(TOKENS):
        at = pl.ds(t, 64, stride=TOKENS)
        d = lax.dot_general(
            vt[at, :].astype(BF16), gt[at, :].astype(BF16), NT, preferred_element_type=F32
        )
        d_t[t] = d
        stat_t[1, t : t + 1, 0:64] = jnp.sum(e_t[t] * d, axis=0, keepdims=True)
    send_ts("b")
    wait_y(3)
    gather_rows(m["spat3"], 0, vs)

    def dots(n):
        j, keys_at, rows_at, lanes_at = tile_at(n)
        d = lax.dot_general(
            vs[keys_at, :].astype(BF16), gs[rows_at, :].astype(BF16), NT,
            preferred_element_type=F32,
        )
        d_s[j, :, lanes_at] = d
        stat_s[1, pl.ds(j, 1), lanes_at] = jnp.sum(e_s[j, :, lanes_at] * d, axis=0, keepdims=True)

    loop(0, 6, dots)
    send_st("b")

    (moment_s,) = got_s("b", 1)
    delta_t = stat_t[1, 0:24, 0:64] * scale_t + moment_s * other_t
    for t in range(TOKENS):
        at = pl.ds(t, 64, stride=TOKENS)
        slope = (p_t[t].astype(F32) * (d_t[t] - delta_t[t : t + 1])).astype(BF16)
        k = kt[at, :].astype(BF16)
        q = qt[at, :].astype(BF16)
        kt[at, :] = jnp.dot(slope, q, preferred_element_type=F32) * SCALE
        across = slope.astype(F32).T.astype(BF16)
        qt[at, :] = jnp.dot(across, k, preferred_element_type=F32) * SCALE

    scatter_rows(qt, m["grad_tk"], 0)
    scatter_rows(kt, m["grad_tk"], 3)
    return_x("k")

    (moment_t,) = got_t("b", 1)
    scale_s[4:6] = stat_s[1, 0:2] * scale_s[0:2] + moment_t * scale_s[2:4]

    def slopes(n):
        j, _, _, lanes_at = tile_at(n)
        gap = d_s[j, :, lanes_at] - scale_s[pl.ds(4 + j, 1), lanes_at]
        sl_s[j, :, lanes_at] = (p_s[j, :, lanes_at].astype(F32) * gap).astype(BF16)

    loop(0, 6, slopes)

    def key_grads(j):
        rows_at = pl.ds(pl.multiple_of(j * ROWS, 8), ROWS)
        q = qs[rows_at, :].astype(BF16)
        k_turned = ks[rows_at, :].T.astype(BF16)
        ks[rows_at, :] = jnp.dot(sl_s[j], q, preferred_element_type=F32) * SCALE
        qs[rows_at, :] = jnp.dot(k_turned, sl_s[j], preferred_element_type=F32).T * SCALE

    loop(0, 2, key_grads)

    scatter_rows(qs, m["grad_sk"], 0)
    scatter_rows(ks, m["grad_sk"], 3)
    return_y("k")
    go_home("k", lambda total, out, to: close_keys(total(0), total(3), out, to))

    wait_home("v")
    restore_values(m["landedv"], dv_out)
    for c in (1, 2, 3):
        drain(c)
    for c in ("a", "b"):
        drain_stats(c)
    drain_back("v")
    wait_home("k")
    restore_keys(m["landedk"], dq_out, dk_out)
    drain_back("k")


def body(queries, keys, values, out_grad, time_bias):
    vmem = pl.BlockSpec(memory_space=pltpu.VMEM)
    shape = jax.ShapeDtypeStruct(queries.shape, BF16)
    shapes = scratch()

    def run(*refs):
        kernel(list(shapes), *refs)

    return pl.pallas_call(
        run,
        out_shape=(shape, shape, shape),
        in_specs=[vmem] * 4 + [pl.BlockSpec(memory_space=pltpu.SMEM)],
        out_specs=(vmem, vmem, vmem),
        scratch_shapes=list(shapes.values()),
        compiler_params=pltpu.CompilerParams(
            collective_id=0, has_side_effects=True, vmem_limit_bytes=56 * 2**20
        ),
    )(queries, keys, values, out_grad, time_bias)


def solution(mesh):
    spec = P("tm", "tok", None)
    return jax.shard_map(
        body, mesh=mesh, in_specs=(spec, spec, spec, spec, P()),
        out_specs=(spec, spec, spec), check_vma=False,
    )
```

```python
import jax
import jax.numpy as jnp
from jax import lax
from jax.experimental import pallas as pl
from jax.experimental.pallas import tpu as pltpu
from jax.sharding import PartitionSpec as P

F32 = jnp.float32
BF16 = jnp.bfloat16
HEADS = 16
DIM = 72
TOKENS = 24
WIDTH = HEADS * DIM
BAND = 8
GROUPS = 32
ROWS = GROUPS * TOKENS
PAIR = 2 * TOKENS
SCALE = DIM**-0.5
NT = (((1,), (1,)), ((), ()))
HIGHEST = lax.Precision.HIGHEST


def device(x, z, core, y):
    return (x * 4 + lax.div(z, 8) * 2 + core, lax.rem(z, 8) * 4 + y)


def lanes_of(rows):
    return lax.broadcasted_iota(jnp.int32, (rows, 128), 1)


def turn(value, shift):
    if isinstance(shift, int):
        shift %= 128
        return value if shift == 0 else pltpu.roll(value, shift, 1)
    return pltpu.roll(value, lax.rem(shift + 256, 128), 1)


def group(value, r):
    return value[16 * r : 16 * r + 16]


def head_run(ref, pair, head):
    first, offset = head * DIM // 128, head * DIM % 128
    tile = [
        jnp.concatenate(
            [ref[2 * pair + j, :, 128 * t : 128 * t + 128].astype(F32) for j in range(2)], axis=0
        )
        for t in range(first, first + (2 if offset + DIM > 128 else 1))
    ]
    if len(tile) == 1:
        return tile[0], offset
    return jnp.where(lanes_of(PAIR) >= offset, tile[0], tile[1]), offset


def pack_first(q_in, k_in, out):
    lane, lane16 = lanes_of(PAIR), lanes_of(16)
    for head in range(HEADS):
        extra = None
        for pair in range(2):
            q, at = head_run(q_in, pair, head)
            k, _ = head_run(k_in, pair, head)
            k = turn(k, 72 - at)
            main = jnp.where(lane < DIM, turn(q, -at), k).astype(BF16)
            for r in range(3):
                out[head, 4 * pair + r] = group(main, r)
                low = 16 * (3 * pair + r)
                piece = turn(group(k, r), low)
                extra = piece if extra is None else jnp.where(lane16 >= low, piece, extra)
        out[head, 3] = extra.astype(BF16)


def pack_second(g_in, v_in, out_g, out_v):
    lane16 = lanes_of(16)
    half = lane16 < 64
    for head in range(HEADS):
        extra = None
        shared_g, shared_v = [], []
        for pair in range(2):
            g, at = head_run(g_in, pair, head)
            v, _ = head_run(v_in, pair, head)
            g = turn(g, -at)
            v = turn(v, -at - 8)
            out_g[head, 3 * pair] = jnp.where(half, group(g, 0), turn(group(g, 1), 64)).astype(BF16)
            out_v[head, 2 * pair] = jnp.where(half, group(v, 0), turn(group(v, 1), 64)).astype(BF16)
            shared_g.append(group(g, 2))
            shared_v.append(group(v, 2))
            for r in range(3):
                low = 16 * (3 * pair + r)
                piece = turn(group(g, r), low - 64)
                extra = piece if extra is None else jnp.where(lane16 >= low, piece, extra)
                extra = jnp.where(lane16 >= low + 8, turn(group(v, r), low + 16), extra)
        out_g[head, 1] = jnp.where(half, shared_g[0], turn(shared_g[1], 64)).astype(BF16)
        out_v[head, 1] = jnp.where(half, shared_v[0], turn(shared_v[1], 64)).astype(BF16)
        out_g[head, 2] = extra.astype(BF16)


def open_first(plane, wide, source):
    lane = lanes_of(16)
    extra = plane[source, 3].astype(F32)
    for p in range(2):
        for r in range(3):
            main = plane[source, 4 * p + r].astype(F32)
            k = jnp.where(lane >= DIM, main, turn(extra, -48 * p - 16 * r))
            wide[source, p, r] = jnp.where(lane < DIM, main, 0.0).astype(BF16)
            wide[source, p, 3 + r] = turn(k, 56).astype(BF16)


def open_second(plane, wide, source):
    lane = lanes_of(16)
    shared = plane[source, 1].astype(F32)
    extra = plane[source, 2].astype(F32)
    for p in range(2):
        own = plane[source, 3 * p].astype(F32)
        for r, main in enumerate((own, turn(own, 64), turn(shared, 64 * p))):
            tail = jnp.where(lane < DIM, turn(extra, 64 - 48 * p - 16 * r), 0.0)
            wide[source, p, r] = jnp.where(lane < 64, main, tail).astype(BF16)


def open_third(plane, plane_g, wide, source):
    lane = lanes_of(16)
    shared = plane[source, 1].astype(F32)
    extra = plane_g[source, 2].astype(F32)
    for p in range(2):
        own = plane[source, 2 * p].astype(F32)
        for r, main in enumerate((turn(own, 8), turn(own, 72), turn(shared, 8 - 64 * p))):
            head = turn(extra, -8 - 48 * p - 16 * r)
            wide[source, p, r] = jnp.where(lane < 8, head, main).astype(BF16)


def gather_rows(tiles, first, ref):
    def one(i, _):
        value = jnp.concatenate([tiles[i, first + r].astype(F32) for r in range(3)], axis=0)
        for j in range(2):
            at = pl.ds(pl.multiple_of(j * ROWS + i * TOKENS, 8), TOKENS)
            ref[at, :] = value[j * TOKENS : (j + 1) * TOKENS]
        return 0

    lax.fori_loop(0, GROUPS, one, 0, unroll=8)


def scatter_rows(ref, tiles, first):
    def one(i, _):
        value = jnp.concatenate(
            [
                ref[pl.ds(pl.multiple_of(j * ROWS + i * TOKENS, 8), TOKENS), :]
                for j in range(2)
            ],
            axis=0,
        )
        for r in range(3):
            tiles[i, first + r] = group(value, r).astype(BF16)
        return 0

    lax.fori_loop(0, GROUPS, one, 0, unroll=8)


def close_values(dv, out, to):
    lane = lanes_of(16)
    half = lane < 64
    for p in range(2):
        out[to, 3 * p] = jnp.where(half, dv[p][0], turn(dv[p][1], 64)).astype(BF16)
    out[to, 1] = jnp.where(half, dv[0][2], turn(dv[1][2], 64)).astype(BF16)
    extra = None
    for p in range(2):
        for r in range(3):
            low = 16 * (3 * p + r)
            piece = turn(dv[p][r], low - 64)
            extra = piece if extra is None else jnp.where(lane >= low, piece, extra)
    out[to, 2] = extra.astype(BF16)


def close_keys(dq, dk, out, to):
    lane = lanes_of(16)
    extra = None
    for p in range(2):
        for r in range(3):
            low = 16 * (3 * p + r)
            k = turn(dk[p][r], 72)
            out[to, 4 * p + r] = jnp.where(lane < DIM, dq[p][r], k).astype(BF16)
            piece = turn(k, low)
            extra = piece if extra is None else jnp.where(lane >= low, piece, extra)
    out[to, 3] = extra.astype(BF16)


def spread_heads(parts, out, pair):
    lane = lanes_of(PAIR)
    for t in range(WIDTH // 128):
        whole = None
        for head in reversed(range(HEADS)):
            low, high = head * DIM - 128 * t, head * DIM + DIM - 128 * t
            if high <= 0 or low >= 128:
                continue
            whole = parts[head] if whole is None else jnp.where(lane < high, parts[head], whole)
        for j in range(2):
            out[2 * pair + j, :, 128 * t : 128 * t + 128] = whole[
                TOKENS * j : TOKENS * j + TOKENS
            ].astype(BF16)


def restore_values(landed, dv_out):
    for pair in range(2):
        parts = []
        lane = lanes_of(PAIR)
        for head in range(HEADS):
            own = landed[head, 3 * pair].astype(F32)
            shared = landed[head, 1].astype(F32)
            extra = landed[head, 2].astype(F32)
            main = jnp.concatenate([own, turn(own, 64), turn(shared, 64 * pair)], axis=0)
            tail = jnp.concatenate(
                [turn(extra, 64 - 48 * pair - 16 * r) for r in range(3)], axis=0
            )
            parts.append(turn(jnp.where(lane < 64, main, tail), head * DIM))
        spread_heads(parts, dv_out, pair)


def restore_keys(landed, dq_out, dk_out):
    for pair in range(2):
        lane = lanes_of(PAIR)
        q_parts, k_parts = [], []
        for head in range(HEADS):
            main = jnp.concatenate(
                [landed[head, 4 * pair + r].astype(F32) for r in range(3)], axis=0
            )
            extra = landed[head, 3].astype(F32)
            extra = jnp.concatenate([turn(extra, -48 * pair - 16 * r) for r in range(3)], axis=0)
            q_parts.append(turn(main, head * DIM))
            k_parts.append(turn(jnp.where(lane >= DIM, main, extra), head * DIM - DIM))
        spread_heads(q_parts, dq_out, pair)
        spread_heads(k_parts, dk_out, pair)


def far_step(n):
    return jnp.where(lax.rem(n, 2) == 1, 8 + lax.div(n, 2), 8 - lax.div(n, 2))


def scratch():
    dma = pltpu.SemaphoreType.DMA

    def tiles(blocks, count):
        return pltpu.VMEM((blocks, count, 16, 128), BF16)

    wide = pltpu.VMEM((2 * ROWS, 128), F32)
    square = (2, ROWS, ROWS)
    small = (TOKENS, 64, 64)
    shapes = {}
    for n, (whole, part) in {1: (7, 6), 2: (4, 3), 3: (3, 3)}.items():
        shapes[f"send{n}"] = tiles(16, whole)
        shapes[f"plane{n}"] = tiles(16, whole)
        shapes[f"wide{n}"] = pltpu.VMEM((16, 2, part, 16, 128), BF16)
        shapes[f"temp{n}"] = tiles(32, part)
        shapes[f"spat{n}"] = tiles(32, part)
        shapes[f"zr{n}"] = dma((16,))
        for name in ("zs", "xs", "xr", "ys", "yr"):
            shapes[f"{name}{n}"] = dma
    for n, (whole, part) in {"v": (4, 3), "k": (7, 6)}.items():
        shapes[f"grad_t{n}"] = tiles(32, part)
        shapes[f"back_t{n}"] = pltpu.VMEM((16, 2, part, 16, 128), BF16)
        shapes[f"final{n}"] = tiles(16, whole)
        shapes[f"landed{n}"] = tiles(16, whole)
        shapes[f"grad_s{n}"] = tiles(32, part)
        shapes[f"back_s{n}"] = tiles(32, part)
        shapes[f"br{n}"] = dma((16,))
        for name in ("bxs", "bys", "bzs", "bzr"):
            shapes[f"{name}{n}"] = dma
    for name in ("qs", "ks", "vs", "gs", "qt", "kt", "vt", "gt"):
        shapes[name] = wide
    shapes.update(
        e_s=pltpu.VMEM(square, F32), d_s=pltpu.VMEM(square, F32),
        p_s=pltpu.VMEM(square, BF16), sl_s=pltpu.VMEM(square, BF16),
        e_t=pltpu.VMEM(small, F32), d_t=pltpu.VMEM(small, F32), p_t=pltpu.VMEM(small, BF16),
        stat_s=pltpu.VMEM((2, 8, ROWS), F32), scale_s=pltpu.VMEM((8, ROWS), F32),
        stat_t=pltpu.VMEM((2, 128, 128), F32),
    )
    for n in ("a", "b"):
        for name in ("to_s", "to_t", "from_s", "from_t"):
            shapes[name + n] = pltpu.VMEM((256, 128), F32)
        for name in ("tss", "tsr", "sts", "str"):
            shapes[name + n] = dma
    return shapes


def kernel(names, q_in, k_in, v_in, g_in, bias_ref, dq_out, dk_out, dv_out, *refs):
    m = dict(zip(names, refs, strict=True))
    tm = lax.axis_index("tm")
    tok = lax.axis_index("tok")
    x, zhi, core = lax.div(tm, 4), lax.rem(lax.div(tm, 2), 2), lax.rem(tm, 2)
    zlo, y = lax.div(tok, 4), lax.rem(tok, 4)
    z = zhi * 8 + zlo
    spot = x * 2 + core
    my_p = lax.rem(y, 2)
    my_pair = x * 8 + lax.div(y, 2) * 4 + core * 2 + my_p
    my_group = y * 8 + spot

    def remote(src, dst, s_sem, r_sem, target):
        return pltpu.make_async_remote_copy(
            src_ref=src, dst_ref=dst, send_sem=s_sem, recv_sem=r_sem,
            device_id=target, device_id_type=pl.DeviceIdType.MESH,
        )

    def start(src, dst, s_sem, r_sem, target, here):
        @pl.when(here)
        def _():
            pltpu.make_async_copy(src, dst, r_sem).start()

        @pl.when(jnp.logical_not(here))
        def _():
            remote(src, dst, s_sem, r_sem, target).start()

    def arrived(ref, sem):
        pltpu.make_async_copy(ref, ref, sem).wait()

    def loop(low, high, step):
        def one(n, _):
            step(n)
            return 0

        lax.fori_loop(low, high, one, 0)

    barrier = pltpu.get_barrier_semaphore()

    def hail(target):
        pl.semaphore_signal(
            barrier, inc=1, device_id=target, device_id_type=pl.DeviceIdType.MESH
        )

    loop(1, 16, lambda n: hail(device(x, lax.rem(z + far_step(n), 16), core, y)))

    def hail_plane(n):
        other = lax.rem(my_group + n, 32)
        there = lax.rem(other, 8)
        hail(device(lax.div(there, 2), z, lax.rem(there, 2), lax.div(other, 8)))

    loop(1, 32, hail_plane)

    def send_line(c):
        send, plane = m[f"send{c}"], m[f"plane{c}"]

        def one(n):
            to = lax.rem(z + far_step(n), 16)
            start(
                send.at[to], plane.at[z], m[f"zs{c}"], m[f"zr{c}"].at[z],
                device(x, to, core, y), to == z,
            )

        loop(1, 17, one)

    pack_first(q_in, k_in, m["send1"])
    pl.semaphore_wait(barrier, 46)
    send_line(1)
    pack_second(g_in, v_in, m["send2"], m["send3"])
    send_line(2)
    send_line(3)

    def forward(c, unpack):
        plane, wide, temp, spat = m[f"plane{c}"], m[f"wide{c}"], m[f"temp{c}"], m[f"spat{c}"]

        def one(n):
            source = lax.rem(z + 16 - far_step(n), 16)
            hi, lo = lax.div(source, 8), lax.rem(source, 8)
            arrived(plane.at[source], m[f"zr{c}"].at[source])
            unpack(source)
            to_x, to_core = lax.div(lo, 2), lax.rem(lo, 2)
            slot = 4 * x + 2 * hi + core
            start(
                wide.at[source], temp.at[pl.ds(pl.multiple_of(2 * slot, 2), 2)],
                m[f"xs{c}"], m[f"xr{c}"],
                device(to_x, z, to_core, y), lo == spot,
            )
            for p in range(2):
                to_y = 2 * hi + p
                start(
                    wide.at[source, p], spat.at[y * 8 + lo],
                    m[f"ys{c}"], m[f"yr{c}"],
                    device(x, z, core, to_y), to_y == y,
                )

        loop(1, 17, one)

    def wait_x(c):
        arrived(m[f"temp{c}"], m[f"xr{c}"])

    def wait_y(c):
        arrived(m[f"spat{c}"], m[f"yr{c}"])

    def send_ts(c):
        to_s, from_t = m["to_s" + c], m["from_t" + c]
        turned = m["stat_t"][0 if c == "a" else 1].T
        to_s[...] = jnp.zeros_like(to_s)
        for j in range(2):
            to_s[pl.ds(j, 32, stride=8), :] = turned[32 * j : 32 * j + 32]

        def one(n):
            r = lax.rem(my_pair + n, 32)
            to_y = 2 * lax.rem(lax.div(r, 4), 2) + lax.rem(r, 2)
            start(
                to_s.at[pl.ds(pl.multiple_of(r * 8, 8), 8)],
                from_t.at[pl.ds(pl.multiple_of(my_group * 8, 8), 8)],
                m["tss" + c], m["tsr" + c],
                device(lax.div(r, 8), z, lax.rem(lax.div(r, 2), 2), to_y), r == my_pair,
            )

        loop(0, 32, one)

    def send_st(c):
        to_t, from_s = m["to_t" + c], m["from_s" + c]
        stat = m["stat_s"][0 if c == "a" else 1]
        row = lax.broadcasted_iota(jnp.int32, (256, ROWS), 0)
        lane = lax.broadcasted_iota(jnp.int32, (256, ROWS), 1)
        own = lax.div(lane, TOKENS) == lax.div(row, 8)
        spread = jnp.where(own, jnp.concatenate([stat] * 32, axis=0), 0.0)
        row = lax.broadcasted_iota(jnp.int32, (ROWS, 128), 0)
        lane = lax.broadcasted_iota(jnp.int32, (ROWS, 128), 1)
        pick = (lax.rem(row, TOKENS) == lane).astype(F32)
        to_t[...] = jnp.dot(spread, pick, precision=HIGHEST, preferred_element_type=F32)

        def one(n):
            i = lax.rem(my_group + n, 32)
            lo = lax.rem(i, 8)
            start(
                to_t.at[pl.ds(pl.multiple_of(i * 8, 8), 8)],
                from_s.at[pl.ds(pl.multiple_of(my_pair * 8, 8), 8)],
                m["sts" + c], m["str" + c],
                device(lax.div(lo, 2), z, lax.rem(lo, 2), lax.div(i, 8)), i == my_group,
            )

        loop(0, 32, one)

    def got_s(c, count):
        from_s = m["from_s" + c]
        arrived(from_s, m["str" + c])
        return [
            jnp.concatenate(
                [from_s[pl.ds(2 * n + j, 32, stride=8), :] for j in range(2)], axis=0
            ).T[0:TOKENS]
            for n in range(count)
        ]

    def got_t(c, count):
        from_t = m["from_t" + c]
        arrived(from_t, m["tsr" + c])
        lane = lax.broadcasted_iota(jnp.int32, (64, ROWS), 1)
        row = lax.broadcasted_iota(jnp.int32, (64, ROWS), 0)
        own = lax.div(lane, TOKENS) == lax.rem(row, 32)
        got = jnp.concatenate([from_t[pl.ds(j, 32, stride=8), :] for j in range(2)], axis=0)
        lane = lax.broadcasted_iota(jnp.int32, (128, ROWS), 1)
        row = lax.broadcasted_iota(jnp.int32, (128, ROWS), 0)
        found = []
        for n in range(count):
            repeat = (lax.rem(lane, TOKENS) == row - TOKENS * n).astype(F32)
            wide = jnp.dot(got, repeat, precision=HIGHEST, preferred_element_type=F32)
            wide = jnp.where(own, wide, 0.0)
            found.append(
                jnp.concatenate(
                    [jnp.sum(wide[32 * j : 32 * j + 32], axis=0, keepdims=True) for j in range(2)],
                    axis=0,
                )
            )
        return found

    def scales(m1, l1, m2, l2):
        top = jnp.maximum(m1, m2)
        a1, a2 = jnp.exp(m1 - top), jnp.exp(m2 - top)
        mass = l1 * a1 + l2 * a2
        return a1 / mass, a2 / mass

    def return_x(c):
        grad, back = m["grad_t" + c], m["back_t" + c]

        def one(n):
            hi, there = lax.rem(n, 2), lax.rem(spot + lax.div(n, 2), 8)
            to_x, to_core = lax.div(there, 2), lax.rem(there, 2)
            source = hi * 8 + spot
            block = pl.ds(pl.multiple_of(2 * (4 * to_x + 2 * hi + to_core), 2), 2)
            start(
                grad.at[block], back.at[source],
                m["bxs" + c], m["br" + c].at[source],
                device(to_x, z, to_core, y), there == spot,
            )

        loop(0, 16, one)

    def return_y(c):
        grad, back = m["grad_s" + c], m["back_s" + c]

        def one(n):
            lo = lax.rem(zlo + far_step(lax.div(n, 4) + 1), 8)
            to_y = lax.rem(y + lax.rem(n, 4), 4)
            start(
                grad.at[to_y * 8 + lo], back.at[y * 8 + lo],
                m["bys" + c], m["br" + c].at[8 * lax.div(y, 2) + lo],
                device(x, z, core, to_y), to_y == y,
            )

        loop(0, 32, one)

    def go_home(c, close):
        back_s, back_t, final = m["back_s" + c], m["back_t" + c], m["final" + c]

        def one(n):
            to = lax.rem(z + far_step(n), 16)
            hi, lo = lax.div(to, 8), lax.rem(to, 8)
            arrived(back_s.at[0:4], m["br" + c].at[to])

            def total(first):
                return [
                    [
                        back_t[to, p, first + r].astype(F32)
                        + back_s[(2 * hi + p) * 8 + lo, first + r].astype(F32)
                        for r in range(3)
                    ]
                    for p in range(2)
                ]

            close(total, final, to)
            start(
                final.at[to], m["landed" + c].at[z], m["bzs" + c], m["bzr" + c],
                device(x, to, core, y), to == z,
            )

        loop(1, 17, one)

    def wait_home(c):
        arrived(m["landed" + c], m["bzr" + c])

    def drain(c):
        arrived(m[f"send{c}"].at[0:15], m[f"zs{c}"])
        arrived(m[f"wide{c}"].at[0:14], m[f"xs{c}"])
        arrived(m[f"spat{c}"].at[0:24], m[f"ys{c}"])

    def drain_back(c):
        arrived(m["final" + c].at[0:15], m["bzs" + c])
        arrived(m["back_t" + c].at[0:14], m["bxs" + c])
        arrived(m["grad_s" + c].at[0:24], m["bys" + c])

    def drain_stats(c):
        arrived(m["to_s" + c].at[0:248], m["tss" + c])
        arrived(m["to_t" + c].at[0:248], m["sts" + c])

    qs, ks, vs, gs = m["qs"], m["ks"], m["vs"], m["gs"]
    qt, kt, vt, gt = m["qt"], m["kt"], m["vt"], m["gt"]
    e_s, d_s, p_s, sl_s = m["e_s"], m["d_s"], m["p_s"], m["sl_s"]
    e_t, d_t, p_t = m["e_t"], m["d_t"], m["p_t"]
    stat_s, stat_t, scale_s = m["stat_s"], m["stat_t"], m["scale_s"]
    stat_s[...] = jnp.zeros_like(stat_s)
    stat_t[...] = jnp.zeros_like(stat_t)

    forward(1, lambda source: open_first(m["plane1"], m["wide1"], source))
    wait_x(1)
    gather_rows(m["temp1"], 0, qt)
    gather_rows(m["temp1"], 3, kt)
    frame_k = lax.broadcasted_iota(jnp.int32, (64, 64), 0)
    frame_q = lax.broadcasted_iota(jnp.int32, (64, 64), 1)
    frame_k = 2 * lax.rem(frame_k, 32) + lax.div(frame_k, 32)
    frame_q = 2 * lax.rem(frame_q, 32) + lax.div(frame_q, 32)
    bias = jnp.full((64, 64), -jnp.inf, F32)
    for j in range(2 * BAND):
        o = j - BAND if j < BAND else j - BAND + 1
        bias = jnp.where(frame_k - frame_q == o, bias_ref[z, j], bias)
    for t in range(TOKENS):
        at = pl.ds(t, 64, stride=TOKENS)
        s = lax.dot_general(
            kt[at, :].astype(BF16), qt[at, :].astype(BF16), NT, preferred_element_type=F32
        ) * SCALE + bias
        top = jnp.max(s, axis=0, keepdims=True)
        e = jnp.exp(s - top)
        e_t[t] = e
        stat_t[0, t : t + 1, 0:64] = top
        stat_t[0, 24 + t : 25 + t, 0:64] = jnp.sum(e, axis=0, keepdims=True)
    send_ts("a")

    wait_y(1)
    gather_rows(m["spat1"], 0, qs)
    gather_rows(m["spat1"], 3, ks)

    def tile_at(n):
        j, b = lax.div(n, 3), lax.rem(n, 3)
        return (
            j,
            pl.ds(pl.multiple_of(j * ROWS, 8), ROWS),
            pl.ds(pl.multiple_of(j * ROWS + b * 256, 8), 256),
            pl.ds(pl.multiple_of(b * 256, 128), 256),
        )

    def scores(n):
        j, keys_at, rows_at, lanes_at = tile_at(n)
        s = lax.dot_general(
            ks[keys_at, :].astype(BF16), qs[rows_at, :].astype(BF16), NT,
            preferred_element_type=F32,
        ) * SCALE
        top = jnp.max(s, axis=0, keepdims=True)
        e = jnp.exp(s - top)
        e_s[j, :, lanes_at] = e
        stat_s[0, pl.ds(j, 1), lanes_at] = top
        stat_s[0, pl.ds(2 + j, 1), lanes_at] = jnp.sum(e, axis=0, keepdims=True)

    loop(0, 6, scores)
    send_st("a")

    forward(2, lambda source: open_second(m["plane2"], m["wide2"], source))
    scale_t, other_t = scales(
        stat_t[0, 0:24, 0:64], stat_t[0, 24:48, 0:64], *got_s("a", 2)
    )
    wait_x(2)
    gather_rows(m["temp2"], 0, gt)
    for t in range(TOKENS):
        at = pl.ds(t, 64, stride=TOKENS)
        rounded = (e_t[t] * scale_t[t : t + 1]).astype(BF16)
        p_t[t] = rounded
        vt[at, :] = jnp.dot(rounded, gt[at, :].astype(BF16), preferred_element_type=F32)

    scatter_rows(vt, m["grad_tv"], 0)
    return_x("v")

    scale_own, scale_other = scales(stat_s[0, 0:2], stat_s[0, 2:4], *got_t("a", 2))
    scale_s[0:2] = scale_own
    scale_s[2:4] = scale_other

    def weights(n):
        j, _, _, lanes_at = tile_at(n)
        p_s[j, :, lanes_at] = (e_s[j, :, lanes_at] * scale_s[pl.ds(j, 1), lanes_at]).astype(BF16)

    loop(0, 6, weights)
    wait_y(2)
    gather_rows(m["spat2"], 0, gs)

    def value_grads(j):
        rows_at = pl.ds(pl.multiple_of(j * ROWS, 8), ROWS)
        vs[rows_at, :] = jnp.dot(
            p_s[j], gs[rows_at, :].astype(BF16), preferred_element_type=F32
        )

    loop(0, 2, value_grads)

    scatter_rows(vs, m["grad_sv"], 0)
    return_y("v")
    forward(3, lambda source: open_third(m["plane3"], m["plane2"], m["wide3"], source))
    go_home("v", lambda total, out, to: close_values(total(0), out, to))

    wait_x(3)
    gather_rows(m["temp3"], 0, vt)
    for t in range(TOKENS):
        at = pl.ds(t, 64, stride=TOKENS)
        d = lax.dot_general(
            vt[at, :].astype(BF16), gt[at, :].astype(BF16), NT, preferred_element_type=F32
        )
        d_t[t] = d
        stat_t[1, t : t + 1, 0:64] = jnp.sum(e_t[t] * d, axis=0, keepdims=True)
    send_ts("b")
    wait_y(3)
    gather_rows(m["spat3"], 0, vs)

    def dots(n):
        j, keys_at, rows_at, lanes_at = tile_at(n)
        d = lax.dot_general(
            vs[keys_at, :].astype(BF16), gs[rows_at, :].astype(BF16), NT,
            preferred_element_type=F32,
        )
        d_s[j, :, lanes_at] = d
        stat_s[1, pl.ds(j, 1), lanes_at] = jnp.sum(e_s[j, :, lanes_at] * d, axis=0, keepdims=True)

    loop(0, 6, dots)
    send_st("b")

    (moment_s,) = got_s("b", 1)
    delta_t = stat_t[1, 0:24, 0:64] * scale_t + moment_s * other_t
    for t in range(TOKENS):
        at = pl.ds(t, 64, stride=TOKENS)
        slope = (p_t[t].astype(F32) * (d_t[t] - delta_t[t : t + 1])).astype(BF16)
        k = kt[at, :].astype(BF16)
        q = qt[at, :].astype(BF16)
        kt[at, :] = jnp.dot(slope, q, preferred_element_type=F32) * SCALE
        across = slope.astype(F32).T.astype(BF16)
        qt[at, :] = jnp.dot(across, k, preferred_element_type=F32) * SCALE

    scatter_rows(qt, m["grad_tk"], 0)
    scatter_rows(kt, m["grad_tk"], 3)
    return_x("k")

    (moment_t,) = got_t("b", 1)
    scale_s[4:6] = stat_s[1, 0:2] * scale_s[0:2] + moment_t * scale_s[2:4]

    def slopes(n):
        j, _, _, lanes_at = tile_at(n)
        gap = d_s[j, :, lanes_at] - scale_s[pl.ds(4 + j, 1), lanes_at]
        sl_s[j, :, lanes_at] = (p_s[j, :, lanes_at].astype(F32) * gap).astype(BF16)

    loop(0, 6, slopes)

    def key_grads(j):
        rows_at = pl.ds(pl.multiple_of(j * ROWS, 8), ROWS)
        q = qs[rows_at, :].astype(BF16)
        k_turned = ks[rows_at, :].T.astype(BF16)
        ks[rows_at, :] = jnp.dot(sl_s[j], q, preferred_element_type=F32) * SCALE
        qs[rows_at, :] = jnp.dot(k_turned, sl_s[j], preferred_element_type=F32).T * SCALE

    loop(0, 2, key_grads)

    scatter_rows(qs, m["grad_sk"], 0)
    scatter_rows(ks, m["grad_sk"], 3)
    return_y("k")
    go_home("k", lambda total, out, to: close_keys(total(0), total(3), out, to))

    wait_home("v")
    restore_values(m["landedv"], dv_out)
    for c in (1, 2, 3):
        drain(c)
    for c in ("a", "b"):
        drain_stats(c)
    drain_back("v")
    wait_home("k")
    restore_keys(m["landedk"], dq_out, dk_out)
    drain_back("k")


def body(queries, keys, values, out_grad, time_bias):
    vmem = pl.BlockSpec(memory_space=pltpu.VMEM)
    shape = jax.ShapeDtypeStruct(queries.shape, BF16)
    shapes = scratch()

    def run(*refs):
        kernel(list(shapes), *refs)

    return pl.pallas_call(
        run,
        out_shape=(shape, shape, shape),
        in_specs=[vmem] * 4 + [pl.BlockSpec(memory_space=pltpu.SMEM)],
        out_specs=(vmem, vmem, vmem),
        scratch_shapes=list(shapes.values()),
        compiler_params=pltpu.CompilerParams(
            collective_id=0, has_side_effects=True, vmem_limit_bytes=56 * 2**20
        ),
    )(queries, keys, values, out_grad, time_bias)


def solution(mesh):
    spec = P("tm", "tok", None)
    return jax.shard_map(
        body, mesh=mesh, in_specs=(spec, spec, spec, spec, P()),
        out_specs=(spec, spec, spec), check_vma=False,
    )
```

```python
import jax
import jax.numpy as jnp
from jax import lax
from jax.experimental import pallas as pl
from jax.experimental.pallas import tpu as pltpu
from jax.sharding import PartitionSpec as P

F32 = jnp.float32
BF16 = jnp.bfloat16
HEADS = 16
DIM = 72
TOKENS = 24
WIDTH = HEADS * DIM
BAND = 8
GROUPS = 32
ROWS = GROUPS * TOKENS
PAIR = 2 * TOKENS
SCALE = DIM**-0.5
NT = (((1,), (1,)), ((), ()))
HIGHEST = lax.Precision.HIGHEST


def device(x, z, core, y):
    return (x * 4 + lax.div(z, 8) * 2 + core, lax.rem(z, 8) * 4 + y)


def lanes_of(rows):
    return lax.broadcasted_iota(jnp.int32, (rows, 128), 1)


def turn(value, shift):
    if isinstance(shift, int):
        shift %= 128
        return value if shift == 0 else pltpu.roll(value, shift, 1)
    return pltpu.roll(value, lax.rem(shift + 256, 128), 1)


def group(value, r):
    return value[16 * r : 16 * r + 16]


def head_run(ref, pair, head):
    first, offset = head * DIM // 128, head * DIM % 128
    tile = [
        jnp.concatenate(
            [ref[2 * pair + j, :, 128 * t : 128 * t + 128].astype(F32) for j in range(2)], axis=0
        )
        for t in range(first, first + (2 if offset + DIM > 128 else 1))
    ]
    if len(tile) == 1:
        return tile[0], offset
    return jnp.where(lanes_of(PAIR) >= offset, tile[0], tile[1]), offset


def pack_first(q_in, k_in, out):
    lane, lane16 = lanes_of(PAIR), lanes_of(16)
    for head in range(HEADS):
        extra = None
        for pair in range(2):
            q, at = head_run(q_in, pair, head)
            k, _ = head_run(k_in, pair, head)
            k = turn(k, 72 - at)
            main = jnp.where(lane < DIM, turn(q, -at), k).astype(BF16)
            for r in range(3):
                out[head, 4 * pair + r] = group(main, r)
                low = 16 * (3 * pair + r)
                piece = turn(group(k, r), low)
                extra = piece if extra is None else jnp.where(lane16 >= low, piece, extra)
        out[head, 3] = extra.astype(BF16)


def pack_second(g_in, v_in, out_g, out_v):
    lane16 = lanes_of(16)
    half = lane16 < 64
    for head in range(HEADS):
        extra = None
        shared_g, shared_v = [], []
        for pair in range(2):
            g, at = head_run(g_in, pair, head)
            v, _ = head_run(v_in, pair, head)
            g = turn(g, -at)
            v = turn(v, -at - 8)
            out_g[head, 3 * pair] = jnp.where(half, group(g, 0), turn(group(g, 1), 64)).astype(BF16)
            out_v[head, 2 * pair] = jnp.where(half, group(v, 0), turn(group(v, 1), 64)).astype(BF16)
            shared_g.append(group(g, 2))
            shared_v.append(group(v, 2))
            for r in range(3):
                low = 16 * (3 * pair + r)
                piece = turn(group(g, r), low - 64)
                extra = piece if extra is None else jnp.where(lane16 >= low, piece, extra)
                extra = jnp.where(lane16 >= low + 8, turn(group(v, r), low + 16), extra)
        out_g[head, 1] = jnp.where(half, shared_g[0], turn(shared_g[1], 64)).astype(BF16)
        out_v[head, 1] = jnp.where(half, shared_v[0], turn(shared_v[1], 64)).astype(BF16)
        out_g[head, 2] = extra.astype(BF16)


def open_first(plane, wide, source):
    lane = lanes_of(16)
    extra = plane[source, 3].astype(F32)
    for p in range(2):
        for r in range(3):
            main = plane[source, 4 * p + r].astype(F32)
            k = jnp.where(lane >= DIM, main, turn(extra, -48 * p - 16 * r))
            wide[source, p, r] = jnp.where(lane < DIM, main, 0.0).astype(BF16)
            wide[source, p, 3 + r] = turn(k, 56).astype(BF16)


def open_second(plane, wide, source):
    lane = lanes_of(16)
    shared = plane[source, 1].astype(F32)
    extra = plane[source, 2].astype(F32)
    for p in range(2):
        own = plane[source, 3 * p].astype(F32)
        for r, main in enumerate((own, turn(own, 64), turn(shared, 64 * p))):
            tail = jnp.where(lane < DIM, turn(extra, 64 - 48 * p - 16 * r), 0.0)
            wide[source, p, r] = jnp.where(lane < 64, main, tail).astype(BF16)


def open_third(plane, plane_g, wide, source):
    lane = lanes_of(16)
    shared = plane[source, 1].astype(F32)
    extra = plane_g[source, 2].astype(F32)
    for p in range(2):
        own = plane[source, 2 * p].astype(F32)
        for r, main in enumerate((turn(own, 8), turn(own, 72), turn(shared, 8 - 64 * p))):
            head = turn(extra, -8 - 48 * p - 16 * r)
            wide[source, p, r] = jnp.where(lane < 8, head, main).astype(BF16)


def gather_rows(tiles, first, ref):
    def one(i, _):
        value = jnp.concatenate([tiles[i, first + r].astype(F32) for r in range(3)], axis=0)
        for j in range(2):
            at = pl.ds(pl.multiple_of(j * ROWS + i * TOKENS, 8), TOKENS)
            ref[at, :] = value[j * TOKENS : (j + 1) * TOKENS]
        return 0

    lax.fori_loop(0, GROUPS, one, 0, unroll=8)


def scatter_rows(ref, tiles, first):
    def one(i, _):
        value = jnp.concatenate(
            [
                ref[pl.ds(pl.multiple_of(j * ROWS + i * TOKENS, 8), TOKENS), :]
                for j in range(2)
            ],
            axis=0,
        )
        for r in range(3):
            tiles[i, first + r] = group(value, r).astype(BF16)
        return 0

    lax.fori_loop(0, GROUPS, one, 0, unroll=8)


def close_values(dv, out, to):
    lane = lanes_of(16)
    half = lane < 64
    for p in range(2):
        out[to, 3 * p] = jnp.where(half, dv[p][0], turn(dv[p][1], 64)).astype(BF16)
    out[to, 1] = jnp.where(half, dv[0][2], turn(dv[1][2], 64)).astype(BF16)
    extra = None
    for p in range(2):
        for r in range(3):
            low = 16 * (3 * p + r)
            piece = turn(dv[p][r], low - 64)
            extra = piece if extra is None else jnp.where(lane >= low, piece, extra)
    out[to, 2] = extra.astype(BF16)


def scatter_keys(q_ref, k_ref, tiles):
    def one(i, _):
        lane, lane16 = lanes_of(PAIR), lanes_of(16)
        dq, dk = (
            jnp.concatenate(
                [
                    ref[pl.ds(pl.multiple_of(j * ROWS + i * TOKENS, 8), TOKENS), :]
                    for j in range(2)
                ],
                axis=0,
            )
            for ref in (q_ref, k_ref)
        )
        dk = turn(dk, 72)
        main = jnp.where(lane < DIM, dq, dk)
        extra = group(dk, 0)
        for r in range(1, 3):
            extra = jnp.where(lane16 >= 16 * r, turn(group(dk, r), 16 * r), extra)
        for r in range(3):
            tiles[i, r] = group(main, r).astype(BF16)
        tiles[i, 3] = extra.astype(BF16)
        return 0

    lax.fori_loop(0, GROUPS, one, 0, unroll=8)


def close_keys(main, extra, out, to):
    lane = lanes_of(16)
    for p in range(2):
        for r in range(3):
            out[to, 4 * p + r] = main[p][r].astype(BF16)
    out[to, 3] = jnp.where(lane < 48, extra[0][0], turn(extra[1][0], 48)).astype(BF16)


def spread_heads(parts, out, pair):
    lane = lanes_of(PAIR)
    for t in range(WIDTH // 128):
        whole = None
        for head in reversed(range(HEADS)):
            low, high = head * DIM - 128 * t, head * DIM + DIM - 128 * t
            if high <= 0 or low >= 128:
                continue
            part = parts[head][...]
            whole = part if whole is None else jnp.where(lane < high, part, whole)
        for j in range(2):
            out[2 * pair + j, :, 128 * t : 128 * t + 128] = whole[
                TOKENS * j : TOKENS * j + TOKENS
            ].astype(BF16)


def restore_values(landed, dv_out):
    for pair in range(2):
        parts = []
        lane = lanes_of(PAIR)
        for head in range(HEADS):
            own = landed[head, 3 * pair].astype(F32)
            shared = landed[head, 1].astype(F32)
            extra = landed[head, 2].astype(F32)
            main = jnp.concatenate([own, turn(own, 64), turn(shared, 64 * pair)], axis=0)
            tail = jnp.concatenate(
                [turn(extra, 64 - 48 * pair - 16 * r) for r in range(3)], axis=0
            )
            parts.append(turn(jnp.where(lane < 64, main, tail), head * DIM))
        spread_heads(parts, dv_out, pair)


def place_keys(landed, q_parts, k_parts, head):
    lane = lanes_of(PAIR)
    extra_tile = landed[head, 3].astype(F32)
    for pair in range(2):
        main = jnp.concatenate(
            [landed[head, 4 * pair + r].astype(F32) for r in range(3)], axis=0
        )
        extra = jnp.concatenate(
            [turn(extra_tile, -48 * pair - 16 * r) for r in range(3)], axis=0
        )
        q_parts[head, pair] = turn(main, head * DIM)
        k_parts[head, pair] = turn(jnp.where(lane >= DIM, main, extra), head * DIM - DIM)


def restore_keys(q_parts, k_parts, dq_out, dk_out):
    for pair in range(2):
        for parts, out in ((q_parts, dq_out), (k_parts, dk_out)):
            spread_heads([parts.at[head, pair] for head in range(HEADS)], out, pair)


def far_step(n):
    return jnp.where(lax.rem(n, 2) == 1, 8 + lax.div(n, 2), 8 - lax.div(n, 2))


def scratch():
    dma = pltpu.SemaphoreType.DMA

    def tiles(blocks, count):
        return pltpu.VMEM((blocks, count, 16, 128), BF16)

    wide = pltpu.VMEM((2 * ROWS, 128), F32)
    square = (2, ROWS, ROWS)
    small = (TOKENS, 64, 64)
    shapes = {}
    for n, (whole, part) in {1: (7, 6), 2: (4, 3), 3: (3, 3)}.items():
        shapes[f"send{n}"] = tiles(16, whole)
        shapes[f"plane{n}"] = tiles(16, whole)
        shapes[f"wide{n}"] = pltpu.VMEM((16, 2, part, 16, 128), BF16)
        shapes[f"temp{n}"] = tiles(32, part)
        shapes[f"spat{n}"] = tiles(32, part)
        shapes[f"zr{n}"] = dma((16,))
        for name in ("zs", "xs", "xr", "ys", "yr"):
            shapes[f"{name}{n}"] = dma
    for n, (whole, part) in {"v": (4, 3), "k": (7, 4)}.items():
        shapes[f"grad_t{n}"] = tiles(32, part)
        shapes[f"back_t{n}"] = pltpu.VMEM((16, 2, part, 16, 128), BF16)
        shapes[f"final{n}"] = tiles(16, whole)
        shapes[f"landed{n}"] = tiles(16, whole)
        shapes[f"grad_s{n}"] = tiles(32, part)
        shapes[f"back_s{n}"] = tiles(32, part)
        shapes[f"br{n}"] = dma((16,))
        for name in ("bxs", "bys", "bzs"):
            shapes[f"{name}{n}"] = dma
    shapes["bzrv"] = dma((1,))
    shapes["bzrk"] = dma((16,))
    for name in ("q_in", "k_in", "v_in", "g_in"):
        shapes[name] = pltpu.VMEM((4, TOKENS, WIDTH), BF16)
    shapes["load"] = dma((4,))
    for name in ("q_parts", "k_parts"):
        shapes[name] = pltpu.VMEM((HEADS, 2, PAIR, 128), F32)
    for name in ("qs", "ks", "vs", "gs", "qt", "kt", "vt", "gt"):
        shapes[name] = wide
    shapes.update(
        e_s=pltpu.VMEM(square, F32), d_s=pltpu.VMEM(square, F32),
        p_s=pltpu.VMEM(square, BF16), sl_s=pltpu.VMEM(square, BF16),
        e_t=pltpu.VMEM(small, F32), d_t=pltpu.VMEM(small, F32), p_t=pltpu.VMEM(small, BF16),
        stat_s=pltpu.VMEM((2, 8, ROWS), F32), scale_s=pltpu.VMEM((8, ROWS), F32),
        stat_t=pltpu.VMEM((2, 128, 128), F32),
    )
    for n in ("a", "b"):
        for name in ("to_s", "to_t", "from_s", "from_t"):
            shapes[name + n] = pltpu.VMEM((256, 128), F32)
        for name in ("tss", "tsr", "sts", "str"):
            shapes[name + n] = dma
    return shapes


def kernel(names, q_hbm, k_hbm, v_hbm, g_hbm, bias_ref, dq_out, dk_out, dv_out, *refs):
    m = dict(zip(names, refs, strict=True))
    q_in, k_in, v_in, g_in = (m[name] for name in ("q_in", "k_in", "v_in", "g_in"))
    tm = lax.axis_index("tm")
    tok = lax.axis_index("tok")
    x, zhi, core = lax.div(tm, 4), lax.rem(lax.div(tm, 2), 2), lax.rem(tm, 2)
    zlo, y = lax.div(tok, 4), lax.rem(tok, 4)
    z = zhi * 8 + zlo
    spot = x * 2 + core
    my_p = lax.rem(y, 2)
    my_pair = x * 8 + lax.div(y, 2) * 4 + core * 2 + my_p
    my_group = y * 8 + spot

    def remote(src, dst, s_sem, r_sem, target):
        return pltpu.make_async_remote_copy(
            src_ref=src, dst_ref=dst, send_sem=s_sem, recv_sem=r_sem,
            device_id=target, device_id_type=pl.DeviceIdType.MESH,
        )

    def start(src, dst, s_sem, r_sem, target, here):
        @pl.when(here)
        def _():
            pltpu.make_async_copy(src, dst, r_sem).start()

        @pl.when(jnp.logical_not(here))
        def _():
            remote(src, dst, s_sem, r_sem, target).start()

    def arrived(ref, sem):
        pltpu.make_async_copy(ref, ref, sem).wait()

    def loop(low, high, step):
        def one(n, _):
            step(n)
            return 0

        lax.fori_loop(low, high, one, 0)

    barrier = pltpu.get_barrier_semaphore()

    def hail(target):
        pl.semaphore_signal(
            barrier, inc=1, device_id=target, device_id_type=pl.DeviceIdType.MESH
        )

    loop(1, 16, lambda n: hail(device(x, lax.rem(z + far_step(n), 16), core, y)))

    def hail_plane(n):
        other = lax.rem(my_group + n, 32)
        there = lax.rem(other, 8)
        hail(device(lax.div(there, 2), z, lax.rem(there, 2), lax.div(other, 8)))

    loop(1, 32, hail_plane)
    loads = [
        pltpu.make_async_copy(source, target, m["load"].at[n])
        for n, (source, target) in enumerate(
            ((q_hbm, q_in), (k_hbm, k_in), (g_hbm, g_in), (v_hbm, v_in))
        )
    ]
    for load in loads:
        load.start()
    loads[0].wait()
    loads[1].wait()

    def send_line(c):
        send, plane = m[f"send{c}"], m[f"plane{c}"]

        def one(n):
            to = lax.rem(z + far_step(n), 16)
            start(
                send.at[to], plane.at[z], m[f"zs{c}"], m[f"zr{c}"].at[z],
                device(x, to, core, y), to == z,
            )

        loop(1, 17, one)

    pack_first(q_in, k_in, m["send1"])
    pl.semaphore_wait(barrier, 46)
    send_line(1)
    loads[2].wait()
    loads[3].wait()
    pack_second(g_in, v_in, m["send2"], m["send3"])
    send_line(2)
    send_line(3)

    def forward(c, unpack):
        plane, wide, temp, spat = m[f"plane{c}"], m[f"wide{c}"], m[f"temp{c}"], m[f"spat{c}"]

        def one(n):
            source = lax.rem(z + 16 - far_step(n), 16)
            hi, lo = lax.div(source, 8), lax.rem(source, 8)
            arrived(plane.at[source], m[f"zr{c}"].at[source])
            unpack(source)
            to_x, to_core = lax.div(lo, 2), lax.rem(lo, 2)
            slot = 4 * x + 2 * hi + core
            start(
                wide.at[source], temp.at[pl.ds(pl.multiple_of(2 * slot, 2), 2)],
                m[f"xs{c}"], m[f"xr{c}"],
                device(to_x, z, to_core, y), lo == spot,
            )
            for p in range(2):
                to_y = 2 * hi + p
                start(
                    wide.at[source, p], spat.at[y * 8 + lo],
                    m[f"ys{c}"], m[f"yr{c}"],
                    device(x, z, core, to_y), to_y == y,
                )

        loop(1, 17, one)

    def wait_x(c):
        arrived(m[f"temp{c}"], m[f"xr{c}"])

    def wait_y(c):
        arrived(m[f"spat{c}"], m[f"yr{c}"])

    def send_ts(c):
        to_s, from_t = m["to_s" + c], m["from_t" + c]
        turned = m["stat_t"][0 if c == "a" else 1].T
        to_s[...] = jnp.zeros_like(to_s)
        for j in range(2):
            to_s[pl.ds(j, 32, stride=8), :] = turned[32 * j : 32 * j + 32]

        def one(n):
            r = lax.rem(my_pair + n, 32)
            to_y = 2 * lax.rem(lax.div(r, 4), 2) + lax.rem(r, 2)
            start(
                to_s.at[pl.ds(pl.multiple_of(r * 8, 8), 8)],
                from_t.at[pl.ds(pl.multiple_of(my_group * 8, 8), 8)],
                m["tss" + c], m["tsr" + c],
                device(lax.div(r, 8), z, lax.rem(lax.div(r, 2), 2), to_y), r == my_pair,
            )

        loop(0, 32, one)

    def send_st(c):
        to_t, from_s = m["to_t" + c], m["from_s" + c]
        stat = m["stat_s"][0 if c == "a" else 1]
        row = lax.broadcasted_iota(jnp.int32, (256, ROWS), 0)
        lane = lax.broadcasted_iota(jnp.int32, (256, ROWS), 1)
        own = lax.div(lane, TOKENS) == lax.div(row, 8)
        spread = jnp.where(own, jnp.concatenate([stat] * 32, axis=0), 0.0)
        row = lax.broadcasted_iota(jnp.int32, (ROWS, 128), 0)
        lane = lax.broadcasted_iota(jnp.int32, (ROWS, 128), 1)
        pick = (lax.rem(row, TOKENS) == lane).astype(F32)
        to_t[...] = jnp.dot(spread, pick, precision=HIGHEST, preferred_element_type=F32)

        def one(n):
            i = lax.rem(my_group + n, 32)
            lo = lax.rem(i, 8)
            start(
                to_t.at[pl.ds(pl.multiple_of(i * 8, 8), 8)],
                from_s.at[pl.ds(pl.multiple_of(my_pair * 8, 8), 8)],
                m["sts" + c], m["str" + c],
                device(lax.div(lo, 2), z, lax.rem(lo, 2), lax.div(i, 8)), i == my_group,
            )

        loop(0, 32, one)

    def got_s(c, count):
        from_s = m["from_s" + c]
        arrived(from_s, m["str" + c])
        return [
            jnp.concatenate(
                [from_s[pl.ds(2 * n + j, 32, stride=8), :] for j in range(2)], axis=0
            ).T[0:TOKENS]
            for n in range(count)
        ]

    def got_t(c, count):
        from_t = m["from_t" + c]
        arrived(from_t, m["tsr" + c])
        lane = lax.broadcasted_iota(jnp.int32, (64, ROWS), 1)
        row = lax.broadcasted_iota(jnp.int32, (64, ROWS), 0)
        own = lax.div(lane, TOKENS) == lax.rem(row, 32)
        got = jnp.concatenate([from_t[pl.ds(j, 32, stride=8), :] for j in range(2)], axis=0)
        lane = lax.broadcasted_iota(jnp.int32, (128, ROWS), 1)
        row = lax.broadcasted_iota(jnp.int32, (128, ROWS), 0)
        found = []
        for n in range(count):
            repeat = (lax.rem(lane, TOKENS) == row - TOKENS * n).astype(F32)
            wide = jnp.dot(got, repeat, precision=HIGHEST, preferred_element_type=F32)
            wide = jnp.where(own, wide, 0.0)
            found.append(
                jnp.concatenate(
                    [jnp.sum(wide[32 * j : 32 * j + 32], axis=0, keepdims=True) for j in range(2)],
                    axis=0,
                )
            )
        return found

    def scales(m1, l1, m2, l2):
        top = jnp.maximum(m1, m2)
        a1, a2 = jnp.exp(m1 - top), jnp.exp(m2 - top)
        mass = l1 * a1 + l2 * a2
        return a1 / mass, a2 / mass

    def return_x(c):
        grad, back = m["grad_t" + c], m["back_t" + c]

        def one(n):
            hi, there = lax.rem(n, 2), lax.rem(spot + lax.div(n, 2), 8)
            to_x, to_core = lax.div(there, 2), lax.rem(there, 2)
            source = hi * 8 + spot
            block = pl.ds(pl.multiple_of(2 * (4 * to_x + 2 * hi + to_core), 2), 2)
            start(
                grad.at[block], back.at[source],
                m["bxs" + c], m["br" + c].at[source],
                device(to_x, z, to_core, y), there == spot,
            )

        loop(0, 16, one)

    def return_y(c):
        grad, back = m["grad_s" + c], m["back_s" + c]

        def one(n):
            lo = lax.rem(zlo + far_step(lax.div(n, 4) + 1), 8)
            to_y = lax.rem(y + lax.rem(n, 4), 4)
            start(
                grad.at[to_y * 8 + lo], back.at[y * 8 + lo],
                m["bys" + c], m["br" + c].at[8 * lax.div(y, 2) + lo],
                device(x, z, core, to_y), to_y == y,
            )

        loop(0, 32, one)

    def go_home(c, close):
        back_s, back_t, final = m["back_s" + c], m["back_t" + c], m["final" + c]

        def one(n):
            to = lax.rem(z + far_step(n), 16)
            hi, lo = lax.div(to, 8), lax.rem(to, 8)
            arrived(back_s.at[0:4], m["br" + c].at[to])

            def total(first, count):
                return [
                    [
                        back_t[to, p, first + r].astype(F32)
                        + back_s[(2 * hi + p) * 8 + lo, first + r].astype(F32)
                        for r in range(count)
                    ]
                    for p in range(2)
                ]

            close(total, final, to)
            start(
                final.at[to], m["landed" + c].at[z], m["bzs" + c], m["bzr" + c].at[z if c == "k" else 0],
                device(x, to, core, y), to == z,
            )

        loop(1, 17, one)

    def home_keys(n):
        head = lax.rem(z + 16 - far_step(n), 16)
        arrived(m["landedk"].at[head], m["bzrk"].at[head])
        place_keys(m["landedk"], m["q_parts"], m["k_parts"], head)

    def drain(c):
        arrived(m[f"send{c}"].at[0:15], m[f"zs{c}"])
        arrived(m[f"wide{c}"].at[0:14], m[f"xs{c}"])
        arrived(m[f"spat{c}"].at[0:24], m[f"ys{c}"])

    def drain_back(c):
        arrived(m["final" + c].at[0:15], m["bzs" + c])
        arrived(m["back_t" + c].at[0:14], m["bxs" + c])
        arrived(m["grad_s" + c].at[0:24], m["bys" + c])

    def drain_stats(c):
        arrived(m["to_s" + c].at[0:248], m["tss" + c])
        arrived(m["to_t" + c].at[0:248], m["sts" + c])

    qs, ks, vs, gs = m["qs"], m["ks"], m["vs"], m["gs"]
    qt, kt, vt, gt = m["qt"], m["kt"], m["vt"], m["gt"]
    e_s, d_s, p_s, sl_s = m["e_s"], m["d_s"], m["p_s"], m["sl_s"]
    e_t, d_t, p_t = m["e_t"], m["d_t"], m["p_t"]
    stat_s, stat_t, scale_s = m["stat_s"], m["stat_t"], m["scale_s"]
    stat_s[...] = jnp.zeros_like(stat_s)
    stat_t[...] = jnp.zeros_like(stat_t)

    forward(1, lambda source: open_first(m["plane1"], m["wide1"], source))
    wait_x(1)
    gather_rows(m["temp1"], 0, qt)
    gather_rows(m["temp1"], 3, kt)
    frame_k = lax.broadcasted_iota(jnp.int32, (64, 64), 0)
    frame_q = lax.broadcasted_iota(jnp.int32, (64, 64), 1)
    frame_k = 2 * lax.rem(frame_k, 32) + lax.div(frame_k, 32)
    frame_q = 2 * lax.rem(frame_q, 32) + lax.div(frame_q, 32)
    bias = jnp.full((64, 64), -jnp.inf, F32)
    for j in range(2 * BAND):
        o = j - BAND if j < BAND else j - BAND + 1
        bias = jnp.where(frame_k - frame_q == o, bias_ref[z, j], bias)
    for t in range(TOKENS):
        at = pl.ds(t, 64, stride=TOKENS)
        s = lax.dot_general(
            kt[at, :].astype(BF16), qt[at, :].astype(BF16), NT, preferred_element_type=F32
        ) * SCALE + bias
        top = jnp.max(s, axis=0, keepdims=True)
        e = jnp.exp(s - top)
        e_t[t] = e
        stat_t[0, t : t + 1, 0:64] = top
        stat_t[0, 24 + t : 25 + t, 0:64] = jnp.sum(e, axis=0, keepdims=True)
    send_ts("a")

    wait_y(1)
    gather_rows(m["spat1"], 0, qs)
    gather_rows(m["spat1"], 3, ks)

    def tile_at(n):
        j, b = lax.div(n, 3), lax.rem(n, 3)
        return (
            j,
            pl.ds(pl.multiple_of(j * ROWS, 8), ROWS),
            pl.ds(pl.multiple_of(j * ROWS + b * 256, 8), 256),
            pl.ds(pl.multiple_of(b * 256, 128), 256),
        )

    def scores(n):
        j, keys_at, rows_at, lanes_at = tile_at(n)
        s = lax.dot_general(
            ks[keys_at, :].astype(BF16), qs[rows_at, :].astype(BF16), NT,
            preferred_element_type=F32,
        ) * SCALE
        top = jnp.max(s, axis=0, keepdims=True)
        e = jnp.exp(s - top)
        e_s[j, :, lanes_at] = e
        stat_s[0, pl.ds(j, 1), lanes_at] = top
        stat_s[0, pl.ds(2 + j, 1), lanes_at] = jnp.sum(e, axis=0, keepdims=True)

    loop(0, 6, scores)
    send_st("a")

    forward(2, lambda source: open_second(m["plane2"], m["wide2"], source))
    scale_t, other_t = scales(
        stat_t[0, 0:24, 0:64], stat_t[0, 24:48, 0:64], *got_s("a", 2)
    )
    wait_x(2)
    forward(3, lambda source: open_third(m["plane3"], m["plane2"], m["wide3"], source))
    gather_rows(m["temp2"], 0, gt)
    for t in range(TOKENS):
        at = pl.ds(t, 64, stride=TOKENS)
        rounded = (e_t[t] * scale_t[t : t + 1]).astype(BF16)
        p_t[t] = rounded
        vt[at, :] = jnp.dot(rounded, gt[at, :].astype(BF16), preferred_element_type=F32)

    scatter_rows(vt, m["grad_tv"], 0)
    return_x("v")

    scale_own, scale_other = scales(stat_s[0, 0:2], stat_s[0, 2:4], *got_t("a", 2))
    scale_s[0:2] = scale_own
    scale_s[2:4] = scale_other

    def weights(n):
        j, _, _, lanes_at = tile_at(n)
        p_s[j, :, lanes_at] = (e_s[j, :, lanes_at] * scale_s[pl.ds(j, 1), lanes_at]).astype(BF16)

    loop(0, 6, weights)
    wait_y(2)
    gather_rows(m["spat2"], 0, gs)

    def value_grads(j):
        rows_at = pl.ds(pl.multiple_of(j * ROWS, 8), ROWS)
        vs[rows_at, :] = jnp.dot(
            p_s[j], gs[rows_at, :].astype(BF16), preferred_element_type=F32
        )

    loop(0, 2, value_grads)

    scatter_rows(vs, m["grad_sv"], 0)
    return_y("v")

    wait_x(3)
    gather_rows(m["temp3"], 0, vt)
    for t in range(TOKENS):
        at = pl.ds(t, 64, stride=TOKENS)
        d = lax.dot_general(
            vt[at, :].astype(BF16), gt[at, :].astype(BF16), NT, preferred_element_type=F32
        )
        d_t[t] = d
        stat_t[1, t : t + 1, 0:64] = jnp.sum(e_t[t] * d, axis=0, keepdims=True)
    send_ts("b")
    wait_y(3)
    gather_rows(m["spat3"], 0, vs)

    def dots(n):
        j, keys_at, rows_at, lanes_at = tile_at(n)
        d = lax.dot_general(
            vs[keys_at, :].astype(BF16), gs[rows_at, :].astype(BF16), NT,
            preferred_element_type=F32,
        )
        d_s[j, :, lanes_at] = d
        stat_s[1, pl.ds(j, 1), lanes_at] = jnp.sum(e_s[j, :, lanes_at] * d, axis=0, keepdims=True)

    loop(0, 6, dots)
    send_st("b")
    go_home("v", lambda total, out, to: close_values(total(0, 3), out, to))

    (moment_s,) = got_s("b", 1)
    delta_t = stat_t[1, 0:24, 0:64] * scale_t + moment_s * other_t
    for t in range(TOKENS):
        at = pl.ds(t, 64, stride=TOKENS)
        slope = (p_t[t].astype(F32) * (d_t[t] - delta_t[t : t + 1])).astype(BF16)
        k = kt[at, :].astype(BF16)
        q = qt[at, :].astype(BF16)
        kt[at, :] = jnp.dot(slope, q, preferred_element_type=F32) * SCALE
        across = slope.astype(F32).T.astype(BF16)
        qt[at, :] = jnp.dot(across, k, preferred_element_type=F32) * SCALE

    scatter_keys(qt, kt, m["grad_tk"])
    return_x("k")

    (moment_t,) = got_t("b", 1)
    scale_s[4:6] = stat_s[1, 0:2] * scale_s[0:2] + moment_t * scale_s[2:4]

    def slopes(n):
        j, _, _, lanes_at = tile_at(n)
        gap = d_s[j, :, lanes_at] - scale_s[pl.ds(4 + j, 1), lanes_at]
        sl_s[j, :, lanes_at] = (p_s[j, :, lanes_at].astype(F32) * gap).astype(BF16)

    loop(0, 6, slopes)

    def key_grads(j):
        rows_at = pl.ds(pl.multiple_of(j * ROWS, 8), ROWS)
        q = qs[rows_at, :].astype(BF16)
        k_turned = ks[rows_at, :].T.astype(BF16)
        ks[rows_at, :] = jnp.dot(sl_s[j], q, preferred_element_type=F32) * SCALE
        qs[rows_at, :] = jnp.dot(k_turned, sl_s[j], preferred_element_type=F32).T * SCALE

    loop(0, 2, key_grads)

    scatter_keys(qs, ks, m["grad_sk"])
    return_y("k")
    go_home("k", lambda total, out, to: close_keys(total(0, 3), total(3, 1), out, to))

    arrived(m["landedv"], m["bzrv"].at[0])
    restore_values(m["landedv"], dv_out)
    for c in (1, 2, 3):
        drain(c)
    for c in ("a", "b"):
        drain_stats(c)
    drain_back("v")
    loop(1, 17, home_keys)
    restore_keys(m["q_parts"], m["k_parts"], dq_out, dk_out)
    drain_back("k")


def body(queries, keys, values, out_grad, time_bias):
    vmem = pl.BlockSpec(memory_space=pltpu.VMEM)
    shape = jax.ShapeDtypeStruct(queries.shape, BF16)
    shapes = scratch()

    def run(*refs):
        kernel(list(shapes), *refs)

    return pl.pallas_call(
        run,
        out_shape=tuple(pltpu.VMEM(queries.shape, BF16) for _ in range(3)),
        in_specs=[pl.BlockSpec(memory_space=pl.ANY)] * 4 + [pl.BlockSpec(memory_space=pltpu.SMEM)],
        out_specs=(vmem, vmem, vmem),
        scratch_shapes=list(shapes.values()),
        compiler_params=pltpu.CompilerParams(
            collective_id=0, has_side_effects=True, vmem_limit_bytes=56 * 2**20
        ),
    )(queries, keys, values, out_grad, time_bias)


def solution(mesh):
    spec = P("tm", "tok", None)
    return jax.shard_map(
        body, mesh=mesh, in_specs=(spec, spec, spec, spec, P()),
        out_specs=(spec, spec, spec), check_vma=False,
    )
```

```python
import jax
import jax.numpy as jnp
from jax import lax
from jax.experimental import pallas as pl
from jax.experimental.pallas import tpu as pltpu
from jax.sharding import PartitionSpec as P

F32 = jnp.float32
BF16 = jnp.bfloat16
HEADS = 16
DIM = 72
TOKENS = 24
WIDTH = HEADS * DIM
BAND = 8
GROUPS = 32
ROWS = GROUPS * TOKENS
PAIR = 2 * TOKENS
SCALE = DIM**-0.5
NT = (((1,), (1,)), ((), ()))
HIGHEST = lax.Precision.HIGHEST


def device(x, z, core, y):
    return (x * 4 + lax.div(z, 8) * 2 + core, lax.rem(z, 8) * 4 + y)


def lanes_of(rows):
    return lax.broadcasted_iota(jnp.int32, (rows, 128), 1)


def turn(value, shift):
    if isinstance(shift, int):
        shift %= 128
        return value if shift == 0 else pltpu.roll(value, shift, 1)
    return pltpu.roll(value, lax.rem(shift + 256, 128), 1)


def group(value, r):
    return value[16 * r : 16 * r + 16]


def head_run(ref, pair, head):
    first, offset = head * DIM // 128, head * DIM % 128
    tile = [
        jnp.concatenate(
            [ref[2 * pair + j, :, 128 * t : 128 * t + 128].astype(F32) for j in range(2)], axis=0
        )
        for t in range(first, first + (2 if offset + DIM > 128 else 1))
    ]
    if len(tile) == 1:
        return tile[0], offset
    return jnp.where(lanes_of(PAIR) >= offset, tile[0], tile[1]), offset


def pack_first(q_in, k_in, out):
    lane, lane16 = lanes_of(PAIR), lanes_of(16)
    for head in range(HEADS):
        extra = None
        for pair in range(2):
            q, at = head_run(q_in, pair, head)
            k, _ = head_run(k_in, pair, head)
            k = turn(k, 72 - at)
            main = jnp.where(lane < DIM, turn(q, -at), k).astype(BF16)
            for r in range(3):
                out[head, 4 * pair + r] = group(main, r)
                low = 16 * (3 * pair + r)
                piece = turn(group(k, r), low)
                extra = piece if extra is None else jnp.where(lane16 >= low, piece, extra)
        out[head, 3] = extra.astype(BF16)


def pack_second(g_in, v_in, out_g, out_v):
    lane16 = lanes_of(16)
    half = lane16 < 64
    for head in range(HEADS):
        extra = None
        shared_g, shared_v = [], []
        for pair in range(2):
            g, at = head_run(g_in, pair, head)
            v, _ = head_run(v_in, pair, head)
            g = turn(g, -at)
            v = turn(v, -at - 8)
            out_g[head, 3 * pair] = jnp.where(half, group(g, 0), turn(group(g, 1), 64)).astype(BF16)
            out_v[head, 2 * pair] = jnp.where(half, group(v, 0), turn(group(v, 1), 64)).astype(BF16)
            shared_g.append(group(g, 2))
            shared_v.append(group(v, 2))
            for r in range(3):
                low = 16 * (3 * pair + r)
                piece = turn(group(g, r), low - 64)
                extra = piece if extra is None else jnp.where(lane16 >= low, piece, extra)
                extra = jnp.where(lane16 >= low + 8, turn(group(v, r), low + 16), extra)
        out_g[head, 1] = jnp.where(half, shared_g[0], turn(shared_g[1], 64)).astype(BF16)
        out_v[head, 1] = jnp.where(half, shared_v[0], turn(shared_v[1], 64)).astype(BF16)
        out_g[head, 2] = extra.astype(BF16)


def open_first(plane, wide, source):
    lane = lanes_of(16)
    extra = plane[source, 3].astype(F32)
    for p in range(2):
        for r in range(3):
            main = plane[source, 4 * p + r].astype(F32)
            k = jnp.where(lane >= DIM, main, turn(extra, -48 * p - 16 * r))
            wide[source, p, r] = jnp.where(lane < DIM, main, 0.0).astype(BF16)
            wide[source, p, 3 + r] = turn(k, 56).astype(BF16)


def open_second(plane, wide, source):
    lane = lanes_of(16)
    shared = plane[source, 1].astype(F32)
    extra = plane[source, 2].astype(F32)
    for p in range(2):
        own = plane[source, 3 * p].astype(F32)
        for r, main in enumerate((own, turn(own, 64), turn(shared, 64 * p))):
            tail = jnp.where(lane < DIM, turn(extra, 64 - 48 * p - 16 * r), 0.0)
            wide[source, p, r] = jnp.where(lane < 64, main, tail).astype(BF16)


def open_third(plane, plane_g, wide, source):
    lane = lanes_of(16)
    shared = plane[source, 1].astype(F32)
    extra = plane_g[source, 2].astype(F32)
    for p in range(2):
        own = plane[source, 2 * p].astype(F32)
        for r, main in enumerate((turn(own, 8), turn(own, 72), turn(shared, 8 - 64 * p))):
            head = turn(extra, -8 - 48 * p - 16 * r)
            wide[source, p, r] = jnp.where(lane < 8, head, main).astype(BF16)


def gather_rows(tiles, first, ref):
    def one(i, _):
        value = jnp.concatenate([tiles[i, first + r].astype(F32) for r in range(3)], axis=0)
        for j in range(2):
            at = pl.ds(pl.multiple_of(j * ROWS + i * TOKENS, 8), TOKENS)
            ref[at, :] = value[j * TOKENS : (j + 1) * TOKENS]
        return 0

    lax.fori_loop(0, GROUPS, one, 0, unroll=8)


def scatter_rows(ref, tiles, first):
    def one(i, _):
        value = jnp.concatenate(
            [
                ref[pl.ds(pl.multiple_of(j * ROWS + i * TOKENS, 8), TOKENS), :]
                for j in range(2)
            ],
            axis=0,
        )
        for r in range(3):
            tiles[i, first + r] = group(value, r).astype(BF16)
        return 0

    lax.fori_loop(0, GROUPS, one, 0, unroll=8)


def close_values(dv, out, to):
    lane = lanes_of(16)
    half = lane < 64
    for p in range(2):
        out[to, 3 * p] = jnp.where(half, dv[p][0], turn(dv[p][1], 64)).astype(BF16)
    out[to, 1] = jnp.where(half, dv[0][2], turn(dv[1][2], 64)).astype(BF16)
    extra = None
    for p in range(2):
        for r in range(3):
            low = 16 * (3 * p + r)
            piece = turn(dv[p][r], low - 64)
            extra = piece if extra is None else jnp.where(lane >= low, piece, extra)
    out[to, 2] = extra.astype(BF16)


def scatter_keys(q_ref, k_ref, tiles):
    def one(i, _):
        lane, lane16 = lanes_of(PAIR), lanes_of(16)
        dq, dk = (
            jnp.concatenate(
                [
                    ref[pl.ds(pl.multiple_of(j * ROWS + i * TOKENS, 8), TOKENS), :]
                    for j in range(2)
                ],
                axis=0,
            )
            for ref in (q_ref, k_ref)
        )
        dk = turn(dk, 72)
        main = jnp.where(lane < DIM, dq, dk)
        extra = group(dk, 0)
        for r in range(1, 3):
            extra = jnp.where(lane16 >= 16 * r, turn(group(dk, r), 16 * r), extra)
        for r in range(3):
            tiles[i, r] = group(main, r).astype(BF16)
        tiles[i, 3] = extra.astype(BF16)
        return 0

    lax.fori_loop(0, GROUPS, one, 0, unroll=8)


def close_keys(main, extra, out, to):
    lane = lanes_of(16)
    for p in range(2):
        for r in range(3):
            out[to, 4 * p + r] = main[p][r].astype(BF16)
    out[to, 3] = jnp.where(lane < 48, extra[0][0], turn(extra[1][0], 48)).astype(BF16)


def spread_heads(parts, out, pair):
    lane = lanes_of(PAIR)
    for t in range(WIDTH // 128):
        whole = None
        for head in reversed(range(HEADS)):
            low, high = head * DIM - 128 * t, head * DIM + DIM - 128 * t
            if high <= 0 or low >= 128:
                continue
            part = parts[head][...]
            whole = part if whole is None else jnp.where(lane < high, part, whole)
        for j in range(2):
            out[2 * pair + j, :, 128 * t : 128 * t + 128] = whole[
                TOKENS * j : TOKENS * j + TOKENS
            ].astype(BF16)


def restore_values(landed, dv_out):
    for pair in range(2):
        parts = []
        lane = lanes_of(PAIR)
        for head in range(HEADS):
            own = landed[head, 3 * pair].astype(F32)
            shared = landed[head, 1].astype(F32)
            extra = landed[head, 2].astype(F32)
            main = jnp.concatenate([own, turn(own, 64), turn(shared, 64 * pair)], axis=0)
            tail = jnp.concatenate(
                [turn(extra, 64 - 48 * pair - 16 * r) for r in range(3)], axis=0
            )
            parts.append(turn(jnp.where(lane < 64, main, tail), head * DIM))
        spread_heads(parts, dv_out, pair)


def place_keys(landed, q_parts, k_parts, head):
    lane = lanes_of(PAIR)
    extra_tile = landed[head, 3].astype(F32)
    for pair in range(2):
        main = jnp.concatenate(
            [landed[head, 4 * pair + r].astype(F32) for r in range(3)], axis=0
        )
        extra = jnp.concatenate(
            [turn(extra_tile, -48 * pair - 16 * r) for r in range(3)], axis=0
        )
        q_parts[head, pair] = turn(main, head * DIM)
        k_parts[head, pair] = turn(jnp.where(lane >= DIM, main, extra), head * DIM - DIM)


def restore_keys(q_parts, k_parts, dq_out, dk_out):
    for pair in range(2):
        for parts, out in ((q_parts, dq_out), (k_parts, dk_out)):
            spread_heads([parts.at[head, pair] for head in range(HEADS)], out, pair)


def far_step(n):
    return jnp.where(lax.rem(n, 2) == 1, 8 + lax.div(n, 2), 8 - lax.div(n, 2))


def scratch():
    dma = pltpu.SemaphoreType.DMA

    def tiles(blocks, count):
        return pltpu.VMEM((blocks, count, 16, 128), BF16)

    wide = pltpu.VMEM((2 * ROWS, 128), F32)
    square = (2, ROWS, ROWS)
    small = (TOKENS, 64, 64)
    shapes = {}
    for n, (whole, part) in {1: (7, 6), 2: (4, 3), 3: (3, 3)}.items():
        shapes[f"send{n}"] = tiles(16, whole)
        shapes[f"plane{n}"] = tiles(16, whole)
        shapes[f"wide{n}"] = pltpu.VMEM((16, 2, part, 16, 128), BF16)
        shapes[f"temp{n}"] = tiles(32, part)
        shapes[f"spat{n}"] = tiles(32, part)
        shapes[f"zr{n}"] = dma((16,))
        for name in ("zs", "xs", "xr", "ys", "yr"):
            shapes[f"{name}{n}"] = dma
    for n, (whole, part) in {"v": (4, 3), "k": (7, 4)}.items():
        shapes[f"grad_t{n}"] = tiles(32, part)
        shapes[f"back_t{n}"] = pltpu.VMEM((16, 2, part, 16, 128), BF16)
        shapes[f"final{n}"] = tiles(16, whole)
        shapes[f"landed{n}"] = tiles(16, whole)
        shapes[f"grad_s{n}"] = tiles(32, part)
        shapes[f"back_s{n}"] = tiles(32, part)
        shapes[f"br{n}"] = dma((16,))
        for name in ("bxs", "bys", "bzs"):
            shapes[f"{name}{n}"] = dma
    shapes["bzrv"] = dma((1,))
    shapes["bzrk"] = dma((16,))
    for name in ("q_in", "k_in", "v_in", "g_in"):
        shapes[name] = pltpu.VMEM((4, TOKENS, WIDTH), BF16)
    shapes["load"] = dma((4,))
    for name in ("q_parts", "k_parts"):
        shapes[name] = pltpu.VMEM((HEADS, 2, PAIR, 128), F32)
    for name in ("qs", "ks", "vs", "gs", "qt", "kt", "vt", "gt"):
        shapes[name] = wide
    shapes.update(
        e_s=pltpu.VMEM(square, F32), d_s=pltpu.VMEM(square, F32),
        p_s=pltpu.VMEM(square, BF16), sl_s=pltpu.VMEM(square, BF16),
        e_t=pltpu.VMEM(small, F32), d_t=pltpu.VMEM(small, F32), p_t=pltpu.VMEM(small, BF16),
        stat_s=pltpu.VMEM((2, 8, ROWS), F32), scale_s=pltpu.VMEM((8, ROWS), F32),
        stat_t=pltpu.VMEM((2, 128, 128), F32),
        own_wide=pltpu.VMEM((256, ROWS), F32), own=pltpu.VMEM((64, ROWS), F32),
        pick=pltpu.VMEM((ROWS, 128), F32), repeat=pltpu.VMEM((2, 128, ROWS), F32),
    )
    for n in ("a", "b"):
        for name in ("to_s", "to_t", "from_s", "from_t"):
            shapes[name + n] = pltpu.VMEM((256, 128), F32)
        for name in ("tss", "tsr", "sts", "str"):
            shapes[name + n] = dma
    return shapes


def kernel(names, q_hbm, k_hbm, v_hbm, g_hbm, bias_ref, dq_out, dk_out, dv_out, *refs):
    m = dict(zip(names, refs, strict=True))
    q_in, k_in, v_in, g_in = (m[name] for name in ("q_in", "k_in", "v_in", "g_in"))
    tm = lax.axis_index("tm")
    tok = lax.axis_index("tok")
    x, zhi, core = lax.div(tm, 4), lax.rem(lax.div(tm, 2), 2), lax.rem(tm, 2)
    zlo, y = lax.div(tok, 4), lax.rem(tok, 4)
    z = zhi * 8 + zlo
    spot = x * 2 + core
    my_p = lax.rem(y, 2)
    my_pair = x * 8 + lax.div(y, 2) * 4 + core * 2 + my_p
    my_group = y * 8 + spot

    def remote(src, dst, s_sem, r_sem, target):
        return pltpu.make_async_remote_copy(
            src_ref=src, dst_ref=dst, send_sem=s_sem, recv_sem=r_sem,
            device_id=target, device_id_type=pl.DeviceIdType.MESH,
        )

    def start(src, dst, s_sem, r_sem, target, here):
        @pl.when(here)
        def _():
            pltpu.make_async_copy(src, dst, r_sem).start()

        @pl.when(jnp.logical_not(here))
        def _():
            remote(src, dst, s_sem, r_sem, target).start()

    def arrived(ref, sem):
        pltpu.make_async_copy(ref, ref, sem).wait()

    def loop(low, high, step):
        def one(n, _):
            step(n)
            return 0

        lax.fori_loop(low, high, one, 0)

    barrier = pltpu.get_barrier_semaphore()

    def hail(target):
        pl.semaphore_signal(
            barrier, inc=1, device_id=target, device_id_type=pl.DeviceIdType.MESH
        )

    loop(1, 16, lambda n: hail(device(x, lax.rem(z + far_step(n), 16), core, y)))

    def hail_plane(n):
        other = lax.rem(my_group + n, 32)
        there = lax.rem(other, 8)
        hail(device(lax.div(there, 2), z, lax.rem(there, 2), lax.div(other, 8)))

    loop(1, 32, hail_plane)
    loads = [
        pltpu.make_async_copy(source, target, m["load"].at[n])
        for n, (source, target) in enumerate(
            ((q_hbm, q_in), (k_hbm, k_in), (g_hbm, g_in), (v_hbm, v_in))
        )
    ]
    for load in loads:
        load.start()
    loads[0].wait()
    loads[1].wait()

    def send_line(c):
        send, plane = m[f"send{c}"], m[f"plane{c}"]

        def one(n):
            to = lax.rem(z + far_step(n), 16)
            start(
                send.at[to], plane.at[z], m[f"zs{c}"], m[f"zr{c}"].at[z],
                device(x, to, core, y), to == z,
            )

        loop(1, 17, one)

    def make_masks():
        def place(rows, lanes):
            return (
                lax.broadcasted_iota(jnp.int32, (rows, lanes), 0),
                lax.broadcasted_iota(jnp.int32, (rows, lanes), 1),
            )

        row, lane = place(256, ROWS)
        m["own_wide"][...] = (lax.div(lane, TOKENS) == lax.div(row, 8)).astype(F32)
        row, lane = place(64, ROWS)
        m["own"][...] = (lax.div(lane, TOKENS) == lax.rem(row, 32)).astype(F32)
        row, lane = place(ROWS, 128)
        m["pick"][...] = (lax.rem(row, TOKENS) == lane).astype(F32)
        row, lane = place(128, ROWS)
        for n in range(2):
            m["repeat"][n] = (lax.rem(lane, TOKENS) == row - TOKENS * n).astype(F32)

    pack_first(q_in, k_in, m["send1"])
    make_masks()
    pl.semaphore_wait(barrier, 46)
    send_line(1)
    loads[2].wait()
    loads[3].wait()
    pack_second(g_in, v_in, m["send2"], m["send3"])
    send_line(2)
    send_line(3)

    def forward(c, unpack, step, low=0, high=16):
        plane, wide, temp, spat = m[f"plane{c}"], m[f"wide{c}"], m[f"temp{c}"], m[f"spat{c}"]

        def pass_on(source):
            hi, lo = lax.div(source, 8), lax.rem(source, 8)
            to_x, to_core = lax.div(lo, 2), lax.rem(lo, 2)
            slot = 4 * x + 2 * hi + core
            start(
                wide.at[source], temp.at[pl.ds(pl.multiple_of(2 * slot, 2), 2)],
                m[f"xs{c}"], m[f"xr{c}"],
                device(to_x, z, to_core, y), lo == spot,
            )
            for p in range(2):
                to_y = 2 * hi + p
                start(
                    wide.at[source, p], spat.at[y * 8 + lo],
                    m[f"ys{c}"], m[f"yr{c}"],
                    device(x, z, core, to_y), to_y == y,
                )

        def one(n):
            sources = [lax.rem(z + 16 - far_step(step * n + k + 1), 16) for k in range(step)]
            for source in sources:
                arrived(plane.at[source], m[f"zr{c}"].at[source])
            for source in sources:
                unpack(source)
            for source in sources:
                pass_on(source)

        loop(low // step, high // step, one)

    def wait_x(c):
        arrived(m[f"temp{c}"], m[f"xr{c}"])

    def wait_y(c):
        arrived(m[f"spat{c}"], m[f"yr{c}"])

    def send_ts(c):
        to_s, from_t = m["to_s" + c], m["from_t" + c]
        turned = m["stat_t"][0 if c == "a" else 1].T
        to_s[...] = jnp.zeros_like(to_s)
        for j in range(2):
            to_s[pl.ds(j, 32, stride=8), :] = turned[32 * j : 32 * j + 32]

        landing = from_t.at[pl.ds(pl.multiple_of(my_group * 8, 8), 8)]

        def one(n):
            r = lax.rem(my_pair + n, 32)
            to_y = 2 * lax.rem(lax.div(r, 4), 2) + lax.rem(r, 2)
            remote(
                to_s.at[pl.ds(pl.multiple_of(r * 8, 8), 8)], landing, m["tss" + c], m["tsr" + c],
                device(lax.div(r, 8), z, lax.rem(lax.div(r, 2), 2), to_y),
            ).start()

        loop(1, 32, one)
        here = to_s.at[pl.ds(pl.multiple_of(my_pair * 8, 8), 8)]
        pltpu.make_async_copy(here, landing, m["tsr" + c]).start()

    def send_st(c):
        to_t, from_s = m["to_t" + c], m["from_s" + c]
        stat = m["stat_s"][0 if c == "a" else 1]
        spread = m["own_wide"][...] * jnp.concatenate([stat] * 32, axis=0)
        to_t[...] = jnp.dot(
            spread, m["pick"][...], precision=HIGHEST, preferred_element_type=F32
        )

        landing = from_s.at[pl.ds(pl.multiple_of(my_pair * 8, 8), 8)]

        def one(n):
            i = lax.rem(my_group + n, 32)
            lo = lax.rem(i, 8)
            remote(
                to_t.at[pl.ds(pl.multiple_of(i * 8, 8), 8)], landing, m["sts" + c], m["str" + c],
                device(lax.div(lo, 2), z, lax.rem(lo, 2), lax.div(i, 8)),
            ).start()

        loop(1, 32, one)
        here = to_t.at[pl.ds(pl.multiple_of(my_group * 8, 8), 8)]
        pltpu.make_async_copy(here, landing, m["str" + c]).start()

    def got_s(c, count):
        from_s = m["from_s" + c]
        arrived(from_s, m["str" + c])
        return [
            jnp.concatenate(
                [from_s[pl.ds(2 * n + j, 32, stride=8), :] for j in range(2)], axis=0
            ).T[0:TOKENS]
            for n in range(count)
        ]

    def got_t(c, count):
        from_t = m["from_t" + c]
        arrived(from_t, m["tsr" + c])
        got = jnp.concatenate([from_t[pl.ds(j, 32, stride=8), :] for j in range(2)], axis=0)
        found = []
        for n in range(count):
            wide = jnp.dot(got, m["repeat"][n], precision=HIGHEST, preferred_element_type=F32)
            wide = wide * m["own"][...]
            found.append(
                jnp.concatenate(
                    [jnp.sum(wide[32 * j : 32 * j + 32], axis=0, keepdims=True) for j in range(2)],
                    axis=0,
                )
            )
        return found

    def scales(m1, l1, m2, l2):
        top = jnp.maximum(m1, m2)
        a1, a2 = jnp.exp(m1 - top), jnp.exp(m2 - top)
        mass = l1 * a1 + l2 * a2
        return a1 / mass, a2 / mass

    def return_x(c):
        grad, back = m["grad_t" + c], m["back_t" + c]

        def one(n):
            hi, there = lax.rem(n, 2), lax.rem(spot + lax.div(n, 2), 8)
            to_x, to_core = lax.div(there, 2), lax.rem(there, 2)
            source = hi * 8 + spot
            block = pl.ds(pl.multiple_of(2 * (4 * to_x + 2 * hi + to_core), 2), 2)
            start(
                grad.at[block], back.at[source],
                m["bxs" + c], m["br" + c].at[source],
                device(to_x, z, to_core, y), there == spot,
            )

        loop(0, 16, one)

    def return_y(c):
        grad, back = m["grad_s" + c], m["back_s" + c]

        def one(n):
            lo = lax.rem(zlo + far_step(lax.div(n, 4) + 1), 8)
            to_y = lax.rem(y + lax.rem(n, 4), 4)
            start(
                grad.at[to_y * 8 + lo], back.at[y * 8 + lo],
                m["bys" + c], m["br" + c].at[8 * lax.div(y, 2) + lo],
                device(x, z, core, to_y), to_y == y,
            )

        loop(0, 32, one)

    def go_home(c, close):
        back_s, back_t, final = m["back_s" + c], m["back_t" + c], m["final" + c]

        def one(n):
            to = lax.rem(z + far_step(n), 16)
            hi, lo = lax.div(to, 8), lax.rem(to, 8)
            arrived(back_s.at[0:4], m["br" + c].at[to])

            def total(first, count):
                return [
                    [
                        back_t[to, p, first + r].astype(F32)
                        + back_s[(2 * hi + p) * 8 + lo, first + r].astype(F32)
                        for r in range(count)
                    ]
                    for p in range(2)
                ]

            close(total, final, to)
            start(
                final.at[to], m["landed" + c].at[z], m["bzs" + c], m["bzr" + c].at[z if c == "k" else 0],
                device(x, to, core, y), to == z,
            )

        loop(1, 17, one)

    def home_keys(n):
        head = lax.rem(z + 16 - far_step(n), 16)
        arrived(m["landedk"].at[head], m["bzrk"].at[head])
        place_keys(m["landedk"], m["q_parts"], m["k_parts"], head)

    def drain(c):
        arrived(m[f"send{c}"].at[0:15], m[f"zs{c}"])
        arrived(m[f"wide{c}"].at[0:14], m[f"xs{c}"])
        arrived(m[f"spat{c}"].at[0:24], m[f"ys{c}"])

    def drain_back(c):
        arrived(m["final" + c].at[0:15], m["bzs" + c])
        arrived(m["back_t" + c].at[0:14], m["bxs" + c])
        arrived(m["grad_s" + c].at[0:24], m["bys" + c])

    def drain_stats(c):
        arrived(m["to_s" + c].at[0:248], m["tss" + c])
        arrived(m["to_t" + c].at[0:248], m["sts" + c])

    qs, ks, vs, gs = m["qs"], m["ks"], m["vs"], m["gs"]
    qt, kt, vt, gt = m["qt"], m["kt"], m["vt"], m["gt"]
    e_s, d_s, p_s, sl_s = m["e_s"], m["d_s"], m["p_s"], m["sl_s"]
    e_t, d_t, p_t = m["e_t"], m["d_t"], m["p_t"]
    stat_s, stat_t, scale_s = m["stat_s"], m["stat_t"], m["scale_s"]
    stat_s[...] = jnp.zeros_like(stat_s)
    stat_t[...] = jnp.zeros_like(stat_t)

    forward(1, lambda source: open_first(m["plane1"], m["wide1"], source), 1)
    wait_x(1)
    gather_rows(m["temp1"], 0, qt)
    gather_rows(m["temp1"], 3, kt)
    frame_k = lax.broadcasted_iota(jnp.int32, (64, 64), 0)
    frame_q = lax.broadcasted_iota(jnp.int32, (64, 64), 1)
    frame_k = 2 * lax.rem(frame_k, 32) + lax.div(frame_k, 32)
    frame_q = 2 * lax.rem(frame_q, 32) + lax.div(frame_q, 32)
    bias = jnp.full((64, 64), -jnp.inf, F32)
    for j in range(2 * BAND):
        o = j - BAND if j < BAND else j - BAND + 1
        bias = jnp.where(frame_k - frame_q == o, bias_ref[z, j], bias)
    for t in range(TOKENS):
        at = pl.ds(t, 64, stride=TOKENS)
        s = lax.dot_general(
            kt[at, :].astype(BF16), qt[at, :].astype(BF16), NT, preferred_element_type=F32
        ) * SCALE + bias
        top = jnp.max(s, axis=0, keepdims=True)
        e = jnp.exp(s - top)
        e_t[t] = e
        stat_t[0, t : t + 1, 0:64] = top
        stat_t[0, 24 + t : 25 + t, 0:64] = jnp.sum(e, axis=0, keepdims=True)
    send_ts("a")

    forward(2, lambda source: open_second(m["plane2"], m["wide2"], source), 2, 0, 8)
    wait_y(1)
    gather_rows(m["spat1"], 0, qs)
    gather_rows(m["spat1"], 3, ks)

    def tile_at(n):
        j, b = lax.div(n, 3), lax.rem(n, 3)
        return (
            j,
            pl.ds(pl.multiple_of(j * ROWS, 8), ROWS),
            pl.ds(pl.multiple_of(j * ROWS + b * 256, 8), 256),
            pl.ds(pl.multiple_of(b * 256, 128), 256),
        )

    def scores(n):
        j, keys_at, rows_at, lanes_at = tile_at(n)
        s = lax.dot_general(
            ks[keys_at, :].astype(BF16), qs[rows_at, :].astype(BF16), NT,
            preferred_element_type=F32,
        ) * SCALE
        top = jnp.max(s, axis=0, keepdims=True)
        e = jnp.exp(s - top)
        e_s[j, :, lanes_at] = e
        stat_s[0, pl.ds(j, 1), lanes_at] = top
        stat_s[0, pl.ds(2 + j, 1), lanes_at] = jnp.sum(e, axis=0, keepdims=True)

    loop(0, 6, scores)
    send_st("a")

    forward(2, lambda source: open_second(m["plane2"], m["wide2"], source), 2, 8, 16)
    forward(3, lambda source: open_third(m["plane3"], m["plane2"], m["wide3"], source), 2, 0, 8)
    scale_t, other_t = scales(
        stat_t[0, 0:24, 0:64], stat_t[0, 24:48, 0:64], *got_s("a", 2)
    )
    wait_x(2)
    forward(3, lambda source: open_third(m["plane3"], m["plane2"], m["wide3"], source), 2, 8, 16)
    gather_rows(m["temp2"], 0, gt)
    for t in range(TOKENS):
        at = pl.ds(t, 64, stride=TOKENS)
        rounded = (e_t[t] * scale_t[t : t + 1]).astype(BF16)
        p_t[t] = rounded
        vt[at, :] = jnp.dot(rounded, gt[at, :].astype(BF16), preferred_element_type=F32)

    scatter_rows(vt, m["grad_tv"], 0)
    return_x("v")

    scale_own, scale_other = scales(stat_s[0, 0:2], stat_s[0, 2:4], *got_t("a", 2))
    scale_s[0:2] = scale_own
    scale_s[2:4] = scale_other

    def weights(n):
        j, _, _, lanes_at = tile_at(n)
        p_s[j, :, lanes_at] = (e_s[j, :, lanes_at] * scale_s[pl.ds(j, 1), lanes_at]).astype(BF16)

    loop(0, 6, weights)
    wait_y(2)
    gather_rows(m["spat2"], 0, gs)

    def value_grads(j):
        rows_at = pl.ds(pl.multiple_of(j * ROWS, 8), ROWS)
        vs[rows_at, :] = jnp.dot(
            p_s[j], gs[rows_at, :].astype(BF16), preferred_element_type=F32
        )

    loop(0, 2, value_grads)

    scatter_rows(vs, m["grad_sv"], 0)
    return_y("v")

    wait_x(3)
    gather_rows(m["temp3"], 0, vt)
    for t in range(TOKENS):
        at = pl.ds(t, 64, stride=TOKENS)
        d = lax.dot_general(
            vt[at, :].astype(BF16), gt[at, :].astype(BF16), NT, preferred_element_type=F32
        )
        d_t[t] = d
        stat_t[1, t : t + 1, 0:64] = jnp.sum(e_t[t] * d, axis=0, keepdims=True)
    send_ts("b")
    wait_y(3)
    gather_rows(m["spat3"], 0, vs)

    def dots(n):
        j, keys_at, rows_at, lanes_at = tile_at(n)
        d = lax.dot_general(
            vs[keys_at, :].astype(BF16), gs[rows_at, :].astype(BF16), NT,
            preferred_element_type=F32,
        )
        d_s[j, :, lanes_at] = d
        stat_s[1, pl.ds(j, 1), lanes_at] = jnp.sum(e_s[j, :, lanes_at] * d, axis=0, keepdims=True)

    loop(0, 6, dots)
    send_st("b")
    go_home("v", lambda total, out, to: close_values(total(0, 3), out, to))

    (moment_s,) = got_s("b", 1)
    delta_t = stat_t[1, 0:24, 0:64] * scale_t + moment_s * other_t
    for t in range(TOKENS):
        at = pl.ds(t, 64, stride=TOKENS)
        slope = (p_t[t].astype(F32) * (d_t[t] - delta_t[t : t + 1])).astype(BF16)
        k = kt[at, :].astype(BF16)
        q = qt[at, :].astype(BF16)
        kt[at, :] = jnp.dot(slope, q, preferred_element_type=F32) * SCALE
        across = slope.astype(F32).T.astype(BF16)
        qt[at, :] = jnp.dot(across, k, preferred_element_type=F32) * SCALE

    scatter_keys(qt, kt, m["grad_tk"])
    return_x("k")

    (moment_t,) = got_t("b", 1)
    scale_s[4:6] = stat_s[1, 0:2] * scale_s[0:2] + moment_t * scale_s[2:4]

    def slopes(n):
        j, _, _, lanes_at = tile_at(n)
        gap = d_s[j, :, lanes_at] - scale_s[pl.ds(4 + j, 1), lanes_at]
        sl_s[j, :, lanes_at] = (p_s[j, :, lanes_at].astype(F32) * gap).astype(BF16)

    loop(0, 6, slopes)

    def key_grads(j):
        rows_at = pl.ds(pl.multiple_of(j * ROWS, 8), ROWS)
        q = qs[rows_at, :].astype(BF16)
        k_turned = ks[rows_at, :].T.astype(BF16)
        ks[rows_at, :] = jnp.dot(sl_s[j], q, preferred_element_type=F32) * SCALE
        qs[rows_at, :] = jnp.dot(k_turned, sl_s[j], preferred_element_type=F32).T * SCALE

    loop(0, 2, key_grads)

    scatter_keys(qs, ks, m["grad_sk"])
    return_y("k")
    go_home("k", lambda total, out, to: close_keys(total(0, 3), total(3, 1), out, to))

    arrived(m["landedv"], m["bzrv"].at[0])
    restore_values(m["landedv"], dv_out)
    for c in (1, 2, 3):
        drain(c)
    for c in ("a", "b"):
        drain_stats(c)
    drain_back("v")
    loop(1, 17, home_keys)
    restore_keys(m["q_parts"], m["k_parts"], dq_out, dk_out)
    drain_back("k")


def body(queries, keys, values, out_grad, time_bias):
    vmem = pl.BlockSpec(memory_space=pltpu.VMEM)
    shape = jax.ShapeDtypeStruct(queries.shape, BF16)
    shapes = scratch()

    def run(*refs):
        kernel(list(shapes), *refs)

    return pl.pallas_call(
        run,
        out_shape=tuple(pltpu.VMEM(queries.shape, BF16) for _ in range(3)),
        in_specs=[pl.BlockSpec(memory_space=pl.ANY)] * 4 + [pl.BlockSpec(memory_space=pltpu.SMEM)],
        out_specs=(vmem, vmem, vmem),
        scratch_shapes=list(shapes.values()),
        compiler_params=pltpu.CompilerParams(
            collective_id=0, has_side_effects=True, vmem_limit_bytes=56 * 2**20
        ),
    )(queries, keys, values, out_grad, time_bias)


def solution(mesh):
    spec = P("tm", "tok", None)
    return jax.shard_map(
        body, mesh=mesh, in_specs=(spec, spec, spec, spec, P()),
        out_specs=(spec, spec, spec), check_vma=False,
    )
```
